32 devices in a mesh: cin: 8 (over z, x), cout: 2 (over y), depth: 2 (over core).
Axes of the slice: x: 2, y: 2, z: 4, core: 2. Of those that a mesh axis runs over, the one named last changes fastest.
Arguments:
- features: bfloat16 [8, 512, 4, 128], P(None, 'cin', 'depth'), may hold values from -6 to 6
- kernel: bfloat16 [27, 512, 512], P(None, 'cout', 'cin'), may hold values from -0.0546875 to 0.0546875
- grad_out: bfloat16 [8, 512, 4, 128], P('cin', 'cout', 'depth'), may hold values from -6 to 6
Outputs:
- output: bfloat16 [8, 512, 4, 128], P('cin', 'cout', 'depth')
- input_grad: bfloat16 [8, 512, 4, 128], P('cout', 'cin', 'depth')
- kernel_grad: float32 [27, 512, 512], P(None, 'cout', 'cin')
The draws below stay inside these ranges and needn't reach their ends.
All inputs are finite; a program needn't handle non-finite values.
Results may differ from the reference program's by a relative error of at most 0.001.
Values may be sent and summed in bfloat16 or wider, within the bound.
No kernel may reach another device: no remote copies, remote signals or barrier semaphores. Data moves between devices by JAX's collectives and lax.ppermute only.
A program may use at most 128 MiB of HBM per device.

```python
import math
import jax
import jax.numpy as jnp

CIN = 512
COUT = 512
W = 128
NH = 8
DEP = 4


def steps_of(key, dims, pieces, smallest, largest):
    factor_of = 1.0
    for position, blocks in pieces:
        draws = jax.random.uniform(jax.random.fold_in(jax.random.fold_in(key, 6), position), (blocks,), jnp.float32, smallest / len(pieces), largest / len(pieces))
        factor_of = factor_of * jnp.repeat(jnp.exp(draws), dims[position] // blocks).reshape((-1,) + (1,) * (len(dims) - 1 - position))
    return factor_of


def bell_draw(rng, extent, spread, most, shards=(), dtype=jnp.bfloat16):
    result = jax.random.normal(rng, extent, jnp.float32) * spread
    if len(shards) > 0:
        result = steps_of(rng, extent, shards, -0.22, 0.18) * result
    return jnp.clip(result, min=-most, max=most).astype(dtype)


def setup_inputs(seed: int = 0) -> dict:
    arg_keys = jax.random.split(jax.random.key(seed), 4)
    return {
        "features": bell_draw(arg_keys[0], (NH, CIN, DEP, W), 1.0, 6.0, ((1, 8), (2, 2))),
        "kernel": bell_draw(arg_keys[1], (27, COUT, CIN), (27 * CIN) ** -0.5, 0.0546875, ((1, 2), (2, 8))),
        "grad_out": bell_draw(arg_keys[2], (NH, COUT, DEP, W), 1.0, 6.0, ((0, 8), (1, 2), (2, 2))),
    }


def reference(features, kernel, grad_out):
    feat = features.astype(jnp.float32)
    grad = grad_out.astype(jnp.float32)
    weight = kernel.astype(jnp.float32)
    feat_pad = jnp.pad(feat, ((1, 1), (0, 0), (1, 1), (1, 1)))
    grad_pad = jnp.pad(grad, ((1, 1), (0, 0), (1, 1), (1, 1)))
    output = jnp.zeros((NH, COUT, DEP, W), jnp.float32)
    input_grad = jnp.zeros((NH, CIN, DEP, W), jnp.float32)
    terms = []
    for depth_off in range(3):
        for row_off in range(3):
            for col_off in range(3):
                tap = 9 * depth_off + 3 * row_off + col_off
                shifted = feat_pad[row_off:row_off + NH, :, depth_off:depth_off + DEP, col_off:col_off + W]
                output = output + jnp.einsum('oc,hcdw->hodw', weight[tap], shifted)
                back = grad_pad[2 - row_off:2 - row_off + NH, :, 2 - depth_off:2 - depth_off + DEP, 2 - col_off:2 - col_off + W]
                input_grad = input_grad + jnp.einsum('oc,hodw->hcdw', weight[tap], back)
                terms.append(jnp.einsum('hodw,hcdw->oc', grad, shifted))
    kernel_grad = jnp.stack(terms, axis=0) * (1.0 / math.sqrt(NH * DEP * W))
    return (output.astype(jnp.bfloat16), input_grad.astype(jnp.bfloat16), kernel_grad)
```

```python
import functools
import math

import jax
import jax.numpy as jnp
from jax import lax
from jax.experimental import pallas as pl
from jax.experimental.pallas import tpu as pltpu
from jax.sharding import PartitionSpec as P

F32 = jnp.float32
BF16 = jnp.bfloat16
VMEM_LIMIT = 48 * 1024 * 1024


def ring_of(size):
    return list(range(0, size, 2)) + list(range(size - 1 - size % 2, 0, -2))


def shifted(x, by):
    width = x.shape[1]
    lane = lax.broadcasted_iota(jnp.int32, x.shape, 1)
    edge = 0 if by == 1 else width - 1
    return jnp.where(lane == edge, 0.0, pltpu.roll(x, by % width, 1))


def forward_kernel(rows_ref, feat_ref, weight_ref, ext_ref, part_ref):
    count, layers, chan, width = feat_ref.shape
    slab = layers - 2
    ext_ref[0] = jnp.zeros(ext_ref.shape[1:], BF16)
    ext_ref[count + 1] = jnp.zeros(ext_ref.shape[1:], BF16)

    @pl.loop(0, count)
    def _(h):
        for d in range(layers):
            x = feat_ref[h, d]
            wide = x.astype(F32)
            cols = slice(d * width, (d + 1) * width)
            ext_ref[h + 1, 0:chan, cols] = shifted(wide, 1).astype(BF16)
            ext_ref[h + 1, chan : 2 * chan, cols] = x
            ext_ref[h + 1, 2 * chan : 3 * chan, cols] = shifted(wide, -1).astype(BF16)

    @pl.loop(0, count)
    def _(k):
        row = rows_ref[k]
        total = None
        for a in range(3):
            right = ext_ref[pl.ds(row, 3), :, a * width : (a + slab) * width]
            right = right.reshape(9 * chan, slab * width)
            term = jnp.dot(weight_ref[a], right, preferred_element_type=F32)
            total = term if total is None else total + term
        part_ref[k] = total


def weight_kernel(rows_ref, ext_ref, *refs):
    grads, acc_ref = refs[:-1], refs[-1]
    chan3 = ext_ref.shape[1]
    cells = grads[0].shape[1]
    width = ext_ref.shape[2] - cells
    width = width // 2
    for a in range(3):
        total = None
        for k, g_ref in enumerate(grads):
            right = ext_ref[pl.ds(rows_ref[k], 3), :, a * width : a * width + cells]
            right = right.reshape(3 * chan3, cells)
            term = lax.dot_general(
                g_ref[...], right, (((1,), (1,)), ((), ())), preferred_element_type=F32
            )
            if k == 0:
                acc_ref[a] = term
            else:
                acc_ref[a] += term


def input_kernel(rows_ref, weight_ref, halo_ref, *refs):
    grads, out_ref, pad_ref = refs[:-2], refs[-2], refs[-1]
    count = len(grads)
    chan = out_ref.shape[1]
    cells = out_ref.shape[2]
    width = halo_ref.shape[3]
    slab = cells // width
    pad_ref[0] = jnp.zeros(pad_ref.shape[1:], BF16)
    pad_ref[count + 1] = jnp.zeros(pad_ref.shape[1:], BF16)
    for k, g_ref in enumerate(grads):
        row = rows_ref[k] + 1
        pad_ref[row, :, 0:width] = halo_ref[0, k]
        pad_ref[row, :, width : width + cells] = g_ref[...]
        pad_ref[row, :, width + cells :] = halo_ref[1, k]

    @pl.loop(0, count)
    def _(h):
        total = None
        for a in range(3):
            right = pad_ref[pl.ds(h, 3), :, (2 - a) * width : (2 - a) * width + cells]
            right = right.reshape(3 * right.shape[1], cells)
            term = jnp.dot(weight_ref[a], right, preferred_element_type=F32)
            total = term if total is None else total + term
        for d in range(slab):
            cols = slice(d * width, (d + 1) * width)
            out_ref[h, :, cols] = (
                shifted(total[0:chan, cols], -1)
                + total[chan : 2 * chan, cols]
                + shifted(total[2 * chan : 3 * chan, cols], 1)
            )


def finish_kernel(scale, own_ref, other_ref, out_ref):
    chan = out_ref.shape[2]
    for a in range(3):
        for j in range(9):
            cols = slice(j * chan, (j + 1) * chan)
            out_ref[9 * a + j] = (own_ref[a, :, cols] + other_ref[a, :, cols]) * scale


def call(kernel, out_shape, args, smem=1, scratch=(), flops=0):
    whole = pl.BlockSpec(memory_space=pltpu.VMEM)
    specs = [pl.BlockSpec(memory_space=pltpu.SMEM)] * smem + [whole] * (len(args) - smem)
    outs = jax.tree.map(lambda _: whole, out_shape)
    moved = sum(x.size * x.dtype.itemsize for x in (*args, *jax.tree.leaves(out_shape)))
    return pl.pallas_call(
        kernel,
        out_shape=out_shape,
        in_specs=specs,
        out_specs=outs,
        scratch_shapes=list(scratch),
        compiler_params=pltpu.CompilerParams(vmem_limit_bytes=VMEM_LIMIT),
        cost_estimate=pl.CostEstimate(flops=flops, bytes_accessed=moved, transcendentals=0),
    )(*args)


def neighbours(x_first, x_last, axis):
    size = lax.axis_size(axis)
    if size == 2:
        here = lax.axis_index(axis)
        sent = jnp.where(here == 0, x_last, x_first)
        got = lax.ppermute(sent, axis, [(0, 1), (1, 0)])
        none = jnp.zeros_like(got)
        return jnp.where(here == 0, none, got), jnp.where(here == 0, got, none)
    up = [(i, i + 1) for i in range(size - 1)]
    down = [(j, i) for i, j in up]
    return lax.ppermute(x_last, axis, up), lax.ppermute(x_first, axis, down)


def per_device(features, kernel, grad_out):
    count, chan, slab, width = features.shape
    outs = kernel.shape[1]
    ring_size = lax.axis_size("cin")
    assert count == ring_size and grad_out.shape[0] == 1
    cells = slab * width
    half = ring_size // 2
    ring = ring_of(ring_size)
    fwd = [(ring[i], ring[(i + 1) % ring_size]) for i in range(ring_size)]
    bwd = [(j, i) for i, j in fwd]
    place = [ring.index(i) for i in range(ring_size)]
    table = jnp.array(
        [[ring[(place[i] + k) % ring_size] for k in range(ring_size)] for i in range(ring_size)],
        jnp.int32,
    )
    rows = lax.dynamic_index_in_dim(table, lax.axis_index("cin"), 0, keepdims=False)

    own = grad_out.reshape(outs, cells)
    grads = [None] * ring_size
    grads[0] = own
    f = b = own
    for s in range(1, half):
        f = lax.ppermute(f, "cin", fwd)
        b = lax.ppermute(b, "cin", bwd)
        grads[ring_size - s] = f
        grads[s] = b
    mid = outs // 2
    f = lax.ppermute(f[:mid], "cin", fwd)
    b = lax.ppermute(b[mid:], "cin", bwd)
    grads[half] = jnp.concatenate([f, b], axis=0)

    before, after = neighbours(features[:, :, :1], features[:, :, slab - 1 :], "depth")
    feat = jnp.concatenate([before, features, after], axis=2).transpose(0, 2, 1, 3)
    taps = kernel.reshape(3, 9, outs, chan)
    w_out = taps.transpose(0, 2, 1, 3).reshape(3, outs, 9 * chan)
    flops = 2 * 27 * outs * chan * count * cells
    ext, part = call(
        forward_kernel,
        (
            jax.ShapeDtypeStruct((count + 2, 3 * chan, cells + 2 * width), BF16),
            jax.ShapeDtypeStruct((count, outs, cells), F32),
        ),
        (rows, feat, w_out),
        flops=flops,
    )
    f = lax.ppermute(part[half, :mid], "cin", fwd)
    b = lax.ppermute(part[half, mid:], "cin", bwd)
    f = jnp.concatenate([part[half - 1, :mid] + f, part[half - 1, mid:]])
    b = jnp.concatenate([part[half + 1, :mid], part[half + 1, mid:] + b])
    for s in range(half - 2, -1, -1):
        f = lax.ppermute(f, "cin", fwd)
        b = lax.ppermute(b, "cin", bwd)
        if s:
            f = f + part[s]
            b = b + part[ring_size - s]
    output = (part[0] + f + b).astype(BF16).reshape(1, outs, slab, width)

    acc = call(
        weight_kernel,
        jax.ShapeDtypeStruct((3, outs, 9 * chan), F32),
        (rows, ext, *grads),
        flops=flops,
    )
    scale = 1.0 / math.sqrt(count * cells * lax.axis_size("depth"))
    if lax.axis_size("depth") == 2:
        other = lax.ppermute(acc, "depth", [(0, 1), (1, 0)])
    else:
        other = lax.psum(acc, "depth") - acc
    kernel_grad = call(
        functools.partial(finish_kernel, scale),
        jax.ShapeDtypeStruct((27, outs, chan), F32),
        (acc, other),
        smem=0,
    )

    stack = jnp.stack(grads)
    before, after = neighbours(stack[:, :, :width], stack[:, :, cells - width :], "depth")
    halo = jnp.stack([before, after])
    w_in = (
        kernel.reshape(3, 3, 3, outs, chan)[:, ::-1]
        .transpose(0, 2, 4, 1, 3)
        .reshape(3, 3 * chan, 3 * outs)
    )
    back = call(
        input_kernel,
        jax.ShapeDtypeStruct((count, chan, cells), F32),
        (rows, w_in, halo, *grads),
        scratch=[pltpu.VMEM((count + 2, outs, cells + 2 * width), BF16)],
        flops=flops,
    )
    parts = lax.axis_size("cout")
    if parts == 2:
        here = lax.axis_index("cout")
        halves = back.reshape(2, count // 2, chan, cells)
        mine = jnp.where(here == 0, halves[0], halves[1])
        sent = jnp.where(here == 0, halves[1], halves[0])
        total = mine + lax.ppermute(sent, "cout", [(0, 1), (1, 0)])
    else:
        total = lax.psum_scatter(back, "cout", scatter_dimension=0, tiled=True)
    input_grad = total.astype(BF16).reshape(count // parts, chan, slab, width)
    return (output, input_grad, kernel_grad)


def solution(mesh):
    return jax.shard_map(
        per_device,
        mesh=mesh,
        in_specs=(
            P(None, "cin", "depth", None),
            P(None, "cout", "cin"),
            P("cin", "cout", "depth", None),
        ),
        out_specs=(
            P("cin", "cout", "depth", None),
            P("cout", "cin", "depth", None),
            P(None, "cout", "cin"),
        ),
        check_vma=False,
    )
```

```python
import functools
import math

import jax
import jax.numpy as jnp
from jax import lax
from jax.experimental import pallas as pl
from jax.experimental.pallas import tpu as pltpu
from jax.sharding import PartitionSpec as P

F32 = jnp.float32
BF16 = jnp.bfloat16
VMEM_LIMIT = 8 * 1024 * 1024


def ring_of(size):
    return list(range(0, size, 2)) + list(range(size - 1 - size % 2, 0, -2))


def shifted(x, by):
    width = x.shape[1]
    lane = lax.broadcasted_iota(jnp.int32, x.shape, 1)
    edge = 0 if by == 1 else width - 1
    return jnp.where(lane == edge, 0.0, pltpu.roll(x, by % width, 1))


def extend_kernel(feat_ref, ext_ref):
    count, layers, chan, width = feat_ref.shape
    ext_ref[0] = jnp.zeros(ext_ref.shape[1:], BF16)
    ext_ref[count + 1] = jnp.zeros(ext_ref.shape[1:], BF16)

    @pl.loop(0, count)
    def _(h):
        for d in range(layers):
            x = feat_ref[h, d]
            wide = x.astype(F32)
            cols = slice(d * width, (d + 1) * width)
            ext_ref[h + 1, 0:chan, cols] = shifted(wide, 1).astype(BF16)
            ext_ref[h + 1, chan : 2 * chan, cols] = x
            ext_ref[h + 1, 2 * chan : 3 * chan, cols] = shifted(wide, -1).astype(BF16)


def forward_kernel(offsets, width, rows_ref, ext_ref, weight_ref, *part_refs):
    chan3 = ext_ref.shape[1]
    cells = ext_ref.shape[2] - 2 * width
    for k, part_ref in zip(offsets, part_refs):
        row = rows_ref[k]
        total = None
        for a in range(3):
            right = ext_ref[pl.ds(row, 3), :, a * width : a * width + cells]
            right = right.reshape(3 * chan3, cells)
            term = jnp.dot(weight_ref[a], right, preferred_element_type=F32)
            total = term if total is None else total + term
        part_ref[...] = total


def weight_kernel(offsets, width, first, rows_ref, ext_ref, *refs):
    size = len(offsets)
    grads = refs[:size]
    acc_ref, token_ref = refs[-2:]
    token_ref[...] = jnp.zeros(token_ref.shape, F32)
    chan3 = ext_ref.shape[1]
    cells = grads[0].shape[1]
    for a in range(3):
        for b in range(3):
            part = slice(b * chan3, (b + 1) * chan3)
            total = None if first else refs[size][a, part]
            for k, g_ref in zip(offsets, grads):
                left = ext_ref[rows_ref[k] + b, :, a * width : a * width + cells]
                term = lax.dot_general(
                    left, g_ref[...], (((1,), (1,)), ((), ())), preferred_element_type=F32
                )
                total = term if total is None else total + term
            acc_ref[a, part] = total


def input_kernel(offsets, first, rows_ref, here_ref, weight_ref, halo_ref, *refs):
    size = len(offsets)
    grads = refs[:size]
    acc_ref, token_ref, pad_ref = refs[-3:]
    token_ref[...] = jnp.zeros(token_ref.shape, F32)
    chan, cells = acc_ref.shape[1:]
    width = halo_ref.shape[2]
    outer = here_ref[0]
    if first:
        acc_ref[...] = jnp.zeros(acc_ref.shape, F32)
    else:
        acc_ref[...] = refs[size][...]
    for i, (k, g_ref) in enumerate(zip(offsets, grads)):
        halo = halo_ref[i]
        none = jnp.zeros_like(halo)
        pad_ref[i, :, 0:width] = jnp.where(outer == 0, none, halo)
        pad_ref[i, :, width : width + cells] = g_ref[...]
        pad_ref[i, :, width + cells :] = jnp.where(outer == 0, halo, none)
        for b in range(3):
            total = None
            for a in range(3):
                right = pad_ref[i, :, (2 - a) * width : (2 - a) * width + cells]
                left = weight_ref[a, 3 * b * chan : 3 * (b + 1) * chan]
                term = jnp.dot(left, right, preferred_element_type=F32)
                total = term if total is None else total + term
            row = rows_ref[k] + b
            for d in range(cells // width):
                cols = slice(d * width, (d + 1) * width)
                acc_ref[row, :, cols] += (
                    shifted(total[0:chan, cols], -1)
                    + total[chan : 2 * chan, cols]
                    + shifted(total[2 * chan :, cols], 1)
                )


def power(k):
    whole = k.astype(jnp.int32)
    size = jnp.abs(whole)
    out = jnp.ones(k.shape, F32)
    for i in range(7):
        step = jnp.where(whole > 0, 2.0 ** (2**i), 2.0 ** -(2**i))
        out = out * jnp.where((size >> i) & 1 == 1, step, 1.0)
    return out


def packed(out_ref, at, spot, x):
    rows, cols = x.shape
    most = jnp.max(jnp.max(jnp.abs(x), axis=0, keepdims=True), axis=1, keepdims=True)
    most = jnp.broadcast_to(jnp.maximum(most, 2.0**-100), (8, cols))
    k = 13.0 - jnp.floor(jnp.log2(most))
    out_ref[at : at + rows] = x * power(k)[0:1]
    out_ref[spot : spot + 8] = k


def unpacked(ref, at, rows, spot):
    return ref[at : at + rows] * power(-ref[spot : spot + 8])[0:1]


def relay_kernel(plan, here_ref, *refs):
    ins, outs = refs[: plan["ins"]], list(refs[plan["ins"] :])
    rows_in, sums_in, rows_out, packs = (plan[n] for n in ("rows_in", "sums_in", "rows_out", "packs"))
    parts = ins[:2]
    held = ins[plan["ins"] - plan["tokens"] - plan["held"] : plan["ins"] - plan["tokens"]]
    came, sums = [None, None], [None, None]
    at = 2
    if plan["unpack"]:
        for i in range(2):
            ref = ins[at + i]
            spot = ref.shape[0] - 16
            if rows_in:
                came[i] = unpacked(ref, 0, rows_in, spot).astype(BF16)
            sums[i] = unpacked(ref, rows_in, sums_in, spot + 8)
        at += 2
    else:
        if rows_in:
            came = [ins[at][...], ins[at + 1][...]]
            at += 2
        if sums_in:
            sums = [ins[at][...], ins[at + 1][...]]
    full = parts[0].shape[0]
    mid = full // 2
    if sums_in == 0:
        sums = [parts[0][0:mid], parts[0][mid:]]
    elif sums_in == mid:
        zero = jnp.zeros_like(sums[0])
        sums = [
            parts[0][...] + jnp.concatenate([sums[0], zero], axis=0),
            parts[1][...] + jnp.concatenate([zero, sums[1]], axis=0),
        ]
    else:
        sums = [parts[0][...] + sums[0], parts[1][...] + sums[1]]
    for i in range(2):
        passed = None
        if rows_out:
            passed = came[i][0:rows_out] if i == 0 else came[i][rows_in - rows_out :]
        if packs:
            out_ref = outs.pop(0)
            spot = out_ref.shape[0] - 16
            if rows_out:
                packed(out_ref, 0, spot, passed.astype(F32))
            else:
                out_ref[spot : spot + 8] = jnp.zeros((8, out_ref.shape[1]), F32)
            packed(out_ref, rows_out, spot + 8, sums[i])
        else:
            if rows_out:
                outs.pop(0)[...] = passed
            outs.pop(0)[...] = sums[i]
    if plan["keep"]:
        if rows_in == mid:
            came = [jnp.concatenate(came, axis=0)]
        for row in came:
            outs.pop(0)[...] = row
    if plan["edges"]:
        edge_out = outs.pop(0)
        width = edge_out.shape[2]
        outer = here_ref[0]
        for i, row in enumerate([ref[...] for ref in held] + came):
            cells = row.shape[1]
            edge_out[i] = jnp.where(outer == 0, row[:, cells - width :], row[:, 0:width])


def scale_kernel(scale, own_ref, other_ref, out_ref, token_ref, held_ref, sems):
    token_ref[...] = jnp.zeros(token_ref.shape, F32)
    copies = []
    for a in range(own_ref.shape[0]):
        held_ref[a] = (own_ref[a] + other_ref[a]) * scale
        copies.append(pltpu.make_async_copy(held_ref.at[a], out_ref.at[a], sems.at[a]))
        copies[-1].start()
    for copy in copies:
        copy.wait()


def add_kernel(count, *refs):
    out_ref = refs[-1]
    total = refs[0][...]
    for ref in refs[1:count]:
        total = total + ref[...]
    out_ref[...] = total.astype(BF16)


def call(kernel, out_shape, args, smem=1, scratch=(), alias=None):
    whole = pl.BlockSpec(memory_space=pltpu.VMEM)
    specs = [pl.BlockSpec(memory_space=pltpu.SMEM)] * smem + [whole] * (len(args) - smem)
    outs = jax.tree.map(lambda _: whole, out_shape)
    return pl.pallas_call(
        kernel,
        out_shape=out_shape,
        in_specs=specs,
        out_specs=outs,
        scratch_shapes=list(scratch),
        input_output_aliases=alias or {},
        compiler_params=pltpu.CompilerParams(vmem_limit_bytes=VMEM_LIMIT),
        cost_estimate=pl.CostEstimate(flops=0, bytes_accessed=0, transcendentals=0),
    )(*args)


def per_device(features, kernel, grad_out):
    count, chan, slab, width = features.shape
    outs = kernel.shape[1]
    ring_size = lax.axis_size("cin")
    assert count == ring_size and grad_out.shape[0] == 1 and lax.axis_size("depth") == 2
    cells = slab * width
    half = ring_size // 2
    mid = outs // 2
    ring = ring_of(ring_size)
    fwd = [(ring[i], ring[(i + 1) % ring_size]) for i in range(ring_size)]
    bwd = [(j, i) for i, j in fwd]
    swap = [(0, 1), (1, 0)]
    me = lax.axis_index("cin")
    spot = jnp.where(me % 2 == 0, me // 2, ring_size - 1 - me // 2)
    spots = (spot + lax.iota(jnp.int32, ring_size)) % ring_size
    even = 2 * spots < ring_size + ring_size % 2
    rows = jnp.where(even, 2 * spots, 2 * (ring_size - 1 - spots) + 1)
    here = lax.axis_index("depth")
    core = jnp.full((1,), here, jnp.int32)
    token = jax.ShapeDtypeStruct((8, 128), F32)

    def send(pair):
        return lax.ppermute(pair[0], "cin", fwd), lax.ppermute(pair[1], "cin", bwd)

    grads = [None] * ring_size
    own = lax.optimization_barrier(grad_out.reshape(outs, cells))
    grads[0] = own
    going = send((own, own))

    edge = jnp.where(here == 0, features[:, :, slab - 1 :], features[:, :, :1])
    edge = lax.ppermute(edge, "depth", swap)
    none = jnp.zeros_like(edge)
    feat = [jnp.where(here == 0, none, edge), features, jnp.where(here == 0, edge, none)]
    feat = jnp.concatenate(feat, axis=2).transpose(0, 2, 1, 3)
    taps = kernel.transpose(0, 2, 1).reshape(3, 9 * chan, outs)
    w_out = taps.transpose(0, 2, 1)
    ext = call(
        extend_kernel,
        jax.ShapeDtypeStruct((count + 2, 3 * chan, cells + 2 * width), BF16),
        (feat,),
        smem=0,
    )

    def forward(offsets):
        return call(
            functools.partial(forward_kernel, offsets, width),
            [jax.ShapeDtypeStruct((outs, cells), F32)] * len(offsets),
            (rows, ext, w_out),
        )

    def weight_part(group, acc):
        held = [grads[k] for k in group]
        first = acc is None
        return call(
            functools.partial(weight_kernel, group, width, first),
            [jax.ShapeDtypeStruct((3, 9 * chan, outs), F32), token],
            (rows, ext, *held) if first else (rows, ext, *held, acc),
            alias=None if first else {2 + len(group): 0},
        )

    def input_part(group, halo, back):
        held = [grads[k] for k in group]
        first = back is None
        size = len(group)
        return call(
            functools.partial(input_kernel, group, first),
            [jax.ShapeDtypeStruct((count + 2, chan, cells), F32), token],
            (rows, core, taps, halo, *held) if first else (rows, core, taps, halo, *held, back),
            smem=2,
            scratch=[pltpu.VMEM((size, outs, cells + 2 * width), BF16)],
            alias=None if first else {4 + size: 0},
        )

    grads[ring_size - 1], grads[1] = going
    going = send(going)
    part = forward(list(range(ring_size)))
    grads[ring_size - 2], grads[2] = going
    near = [0, ring_size - 1, 1, ring_size - 2, 2]
    far = [k for k in range(ring_size) if k not in near]

    def slim(r):
        return r < half and 8 * r * r <= 9 * ring_size

    acc = back = None
    tokens = []
    going = (going, None, False)
    for r in range(1, half + 1):
        came, came_sums, unpack = going
        rows_in = 0 if r + 1 > half else mid if r + 1 == half else outs
        rows_out = 0 if r + 2 > half else mid if r + 2 == half else outs
        sums_in = 0 if r == 1 else mid if r == 2 else outs
        sums_out = mid if r == 1 else outs
        packs = slim(r)
        keep = bool(rows_in) and r > 1
        if r == 1:
            group = near
        elif r + 1 == half:
            group = far
        else:
            group = []
        new = [half] if rows_in == mid else [ring_size - r - 1, r + 1]
        held = [k for k in group if k not in new]
        left = half + 1 - r
        ins = [part[left], part[ring_size - left]]
        if unpack:
            ins += [x.astype(F32) for x in came]
        else:
            ins += list(came) if rows_in else []
            ins += list(came_sums) if sums_in else []
        ins += [grads[k] for k in held] + tokens
        if packs:
            shapes = [jax.ShapeDtypeStruct((rows_out + sums_out + 16, cells), F32)] * 2
        else:
            shapes = [jax.ShapeDtypeStruct((rows_out, cells), BF16)] if rows_out else []
            shapes = (shapes + [jax.ShapeDtypeStruct((sums_out, cells), F32)]) * 2
        sent = len(shapes)
        if keep:
            shapes = shapes + [jax.ShapeDtypeStruct((outs, cells), BF16)] * len(new)
        if group:
            shapes = shapes + [jax.ShapeDtypeStruct((len(group), outs, width), BF16)]
        plan = dict(
            ins=len(ins),
            held=len(held),
            tokens=len(tokens),
            rows_in=rows_in,
            sums_in=sums_in,
            rows_out=rows_out,
            packs=packs,
            unpack=unpack,
            keep=keep,
            edges=bool(group),
        )
        made = call(functools.partial(relay_kernel, plan), shapes, (core, *ins))
        if keep:
            for k, row in zip(new, made[sent:]):
                grads[k] = row
        if packs:
            going = (send([x.astype(jnp.float16) for x in made[:2]]), None, True)
        elif rows_out:
            going = (send((made[0], made[2])), send((made[1], made[3])), False)
        else:
            going = (None, send((made[0], made[1])), False)
        tokens = []
        if group:
            group = held + new
            halo = lax.ppermute(made[-1], "depth", swap)
            acc, token_w = weight_part(group, acc)
            back, token_i = input_part(group, halo, back)
            tokens = [token_w, token_i]
    f, b = going[1]

    scale = 1.0 / math.sqrt(count * cells * lax.axis_size("depth"))
    acc_shape = acc.shape
    whole = pl.BlockSpec(memory_space=pltpu.VMEM)
    kernel_grad, token_k = pl.pallas_call(
        functools.partial(scale_kernel, scale),
        out_shape=[jax.ShapeDtypeStruct(acc_shape, F32), token],
        in_specs=[whole, whole],
        out_specs=[pl.BlockSpec(memory_space=pl.ANY), whole],
        scratch_shapes=[pltpu.VMEM(acc_shape, F32), pltpu.SemaphoreType.DMA((acc_shape[0],))],
        compiler_params=pltpu.CompilerParams(vmem_limit_bytes=VMEM_LIMIT),
        cost_estimate=pl.CostEstimate(flops=0, bytes_accessed=0, transcendentals=0),
    )(acc, lax.ppermute(acc, "depth", swap))
    kernel_grad = kernel_grad.reshape(27, chan, outs).transpose(0, 2, 1)
    back = back[1 : count + 1]
    parts = lax.axis_size("cout")
    if parts == 2:
        side = lax.axis_index("cout")
        halves = back.reshape(2, count // 2, chan, cells)
        mine = jnp.where(side == 0, halves[0], halves[1])
        sent = jnp.where(side == 0, halves[1], halves[0])
        terms = [mine, lax.ppermute(sent, "cout", swap)]
    else:
        terms = [lax.psum_scatter(back, "cout", scatter_dimension=0, tiled=True)]
    input_grad = call(
        functools.partial(add_kernel, len(terms)),
        jax.ShapeDtypeStruct((count // parts, chan, cells), BF16),
        (*terms, token_k),
        smem=0,
    )
    output = call(
        functools.partial(add_kernel, 3),
        jax.ShapeDtypeStruct((outs, cells), BF16),
        (part[0], f, b, token_k),
        smem=0,
    )
    input_grad = input_grad.reshape(count // parts, chan, slab, width)
    output = output.reshape(1, outs, slab, width)
    return (output, input_grad, kernel_grad)


def solution(mesh):
    return jax.shard_map(
        per_device,
        mesh=mesh,
        in_specs=(
            P(None, "cin", "depth", None),
            P(None, "cout", "cin"),
            P("cin", "cout", "depth", None),
        ),
        out_specs=(
            P("cin", "cout", "depth", None),
            P("cout", "cin", "depth", None),
            P(None, "cout", "cin"),
        ),
        check_vma=False,
    )
```

```python
import functools
import math

import jax
import jax.numpy as jnp
from jax import lax
from jax.experimental import pallas as pl
from jax.experimental.pallas import tpu as pltpu
from jax.sharding import PartitionSpec as P

F32 = jnp.float32
BF16 = jnp.bfloat16
VMEM_LIMIT = 8 * 1024 * 1024


def ring_of(size):
    return list(range(0, size, 2)) + list(range(size - 1 - size % 2, 0, -2))


def shifted(x, by):
    width = x.shape[1]
    lane = lax.broadcasted_iota(jnp.int32, x.shape, 1)
    edge = 0 if by == 1 else width - 1
    return jnp.where(lane == edge, 0.0, pltpu.roll(x, by % width, 1))


def ring_row(k, size):
    me = lax.axis_index("cin")
    spot = jnp.where(me % 2 == 0, me // 2, size - 1 - me // 2)
    spot = (spot + k) % size
    return jnp.where(2 * spot < size + size % 2, 2 * spot, 2 * (size - 1 - spot) + 1)


def extend_kernel(own, feat_ref, next_ref, ext_ref):
    count, slab, chan, width = feat_ref.shape
    low = lax.axis_index("depth") == (0 if own else 1)
    ext_ref[0] = jnp.zeros(ext_ref.shape[1:], BF16)
    ext_ref[count + 1] = jnp.zeros(ext_ref.shape[1:], BF16)

    @pl.loop(0, count)
    def _(h):
        for d in range(slab + 2):
            if d == 0:
                x = next_ref[h, slab - 1]
                x = jnp.where(low, jnp.zeros_like(x), x)
            elif d == slab + 1:
                x = next_ref[h, 0]
                x = jnp.where(low, x, jnp.zeros_like(x))
            else:
                x = feat_ref[h, d - 1]
            wide = x.astype(F32)
            cols = slice(d * width, (d + 1) * width)
            ext_ref[h + 1, 0:chan, cols] = shifted(wide, 1).astype(BF16)
            ext_ref[h + 1, chan : 2 * chan, cols] = x
            ext_ref[h + 1, 2 * chan : 3 * chan, cols] = shifted(wide, -1).astype(BF16)


def turn_kernel(in_ref, out_ref):
    for a in range(in_ref.shape[0]):
        out_ref[a] = in_ref[a].T


def forward_kernel(offsets, skip, width, ext_ref, weight_ref, *part_refs):
    part_refs = part_refs[skip:]
    chan3 = ext_ref.shape[1]
    cells = ext_ref.shape[2] - 2 * width
    for k, part_ref in zip(offsets, part_refs):
        row = ring_row(k, ext_ref.shape[0] - 2)
        total = None
        for a in range(3):
            right = ext_ref[pl.ds(row, 3), :, a * width : a * width + cells]
            right = right.reshape(3 * chan3, cells)
            term = jnp.dot(weight_ref[a], right, preferred_element_type=F32)
            total = term if total is None else total + term
        part_ref[...] = total


def weight_kernel(groups, width, scale, ext_ref, other_ref, *refs):
    stacks = refs[: 2 * len(groups)]
    out_ref, token_ref, held_ref, sems = refs[-4:]
    token_ref[...] = jnp.zeros(token_ref.shape, F32)
    chan3 = ext_ref.shape[1]
    cells = stacks[0].shape[2]
    terms = []
    for g, group in enumerate(groups):
        for i, k in enumerate(group):
            row = ring_row(k, ext_ref.shape[0] - 2)
            terms.append((row, ext_ref, stacks[g], i))
            terms.append((row, other_ref, stacks[len(groups) + g], i))
    copies = []
    for a in range(3):
        total = None
        for row, source, stack, i in terms:
            left = source[pl.ds(row, 3), :, a * width : a * width + cells]
            term = lax.dot_general(
                left.reshape(3 * chan3, cells),
                stack[i],
                (((1,), (1,)), ((), ())),
                preferred_element_type=F32,
            )
            total = term if total is None else total + term
        held_ref[a] = total * scale
        copies.append(pltpu.make_async_copy(held_ref.at[a], out_ref.at[a], sems.at[a]))
        copies[-1].start()
    for copy in copies:
        copy.wait()


def input_kernel(offsets, first, count, split, weight_ref, theirs_ref, *refs):
    size = len(offsets)
    grads = refs[:size]
    pad_ref = refs[-1]
    if split:
        mine_ref, sent_ref, acc_ref = refs[-4:-1]
    else:
        acc_ref, token_ref = refs[-3:-1]
        token_ref[...] = jnp.zeros(token_ref.shape, F32)
    chan, cells = acc_ref.shape[1:]
    width = (pad_ref.shape[2] - cells) // 2
    low = lax.axis_index("depth") == 0
    if first:
        acc_ref[...] = jnp.zeros(acc_ref.shape, F32)
    else:
        acc_ref[...] = refs[size][...]
    for i, (k, g_ref) in enumerate(zip(offsets, grads)):
        none = jnp.zeros((g_ref.shape[0], width), BF16)
        pad_ref[i, :, 0:width] = jnp.where(low, none, theirs_ref[i, :, cells - width :])
        pad_ref[i, :, width : width + cells] = g_ref[...]
        pad_ref[i, :, width + cells :] = jnp.where(low, theirs_ref[i, :, 0:width], none)
        for b in range(3):
            total = None
            for a in range(3):
                right = pad_ref[i, :, (2 - a) * width : (2 - a) * width + cells]
                left = weight_ref[a, 3 * b * chan : 3 * (b + 1) * chan]
                term = jnp.dot(left, right, preferred_element_type=F32)
                total = term if total is None else total + term
            row = ring_row(k, count) + b
            for d in range(cells // width):
                cols = slice(d * width, (d + 1) * width)
                acc_ref[row, :, cols] += (
                    shifted(total[0:chan, cols], -1)
                    + total[chan : 2 * chan, cols]
                    + shifted(total[2 * chan :, cols], 1)
                )
    if split:
        kept = count // 2
        side = lax.axis_index("cout")
        mine_ref[...] = acc_ref[pl.ds(1 + side * kept, kept)]
        sent_ref[...] = acc_ref[pl.ds(1 + (1 - side) * kept, kept)]


def power(k):
    whole = k.astype(jnp.int32)
    size = jnp.abs(whole)
    out = jnp.ones(k.shape, F32)
    for i in range(7):
        step = jnp.where(whole > 0, 2.0 ** (2**i), 2.0 ** -(2**i))
        out = out * jnp.where((size >> i) & 1 == 1, step, 1.0)
    return out


def packed(out_ref, at, spot, x):
    rows, cols = x.shape
    most = jnp.max(jnp.max(jnp.abs(x), axis=0, keepdims=True), axis=1, keepdims=True)
    most = jnp.broadcast_to(jnp.maximum(most, 2.0**-100), (8, cols))
    k = 13.0 - jnp.floor(jnp.log2(most))
    out_ref[at : at + rows] = x * power(k)[0:1]
    out_ref[spot : spot + 8] = k


def unpacked(ref, at, rows, spot):
    return ref[at : at + rows] * power(-ref[spot : spot + 8])[0:1]


def relay_kernel(plan, part_ref, *refs):
    back, rows_in, sums_in, rows_out = (plan[n] for n in ("back", "rows_in", "sums_in", "rows_out"))
    ins, outs = list(refs[: plan["ins"]]), list(refs[plan["ins"] + plan["skip"] :])
    full = part_ref.shape[0]
    mid = full // 2
    came = total = None
    if plan["raw"]:
        came = ins.pop(0)[...]
    if plan["unpack"]:
        ref = ins.pop(0)
        spot = ref.shape[0] - 16
        held = 0 if plan["raw"] else rows_in
        if held:
            came = unpacked(ref, 0, held, spot).astype(BF16)
        total = unpacked(ref, held, sums_in, spot + 8)
    elif sums_in:
        total = ins.pop(0)[...]
    if sums_in == 0:
        total = part_ref[mid:] if back else part_ref[0:mid]
    elif sums_in == mid:
        pair = [total, jnp.zeros_like(total)]
        total = part_ref[...] + jnp.concatenate(pair[::-1] if back else pair, axis=0)
    else:
        total = part_ref[...] + total
    if rows_out:
        passed = came[rows_in - rows_out :] if back else came[0:rows_out]
        if plan["apart"]:
            outs.pop(0)[...] = passed
            rows_out = 0
    if plan["packs"]:
        out_ref = outs.pop(0)
        spot = out_ref.shape[0] - 16
        if rows_out:
            packed(out_ref, 0, spot, passed.astype(F32))
        else:
            out_ref[spot : spot + 8] = jnp.zeros((8, out_ref.shape[1]), F32)
        packed(out_ref, rows_out, spot + 8, total)
    else:
        outs.pop(0)[...] = total
    if outs:
        outs.pop(0)[...] = came


def stack_kernel(count, *refs):
    out_ref = refs[-1]
    for i in range(count):
        out_ref[i] = refs[i][...]


def join_kernel(first_ref, second_ref, out_ref):
    mid = first_ref.shape[0]
    out_ref[0:mid] = first_ref[...]
    out_ref[mid:] = second_ref[...]


def add_kernel(count, *refs):
    out_ref, token_ref = refs[-2:]
    token_ref[...] = jnp.zeros(token_ref.shape, F32)
    total = refs[0][...]
    for ref in refs[1:count]:
        total = total + ref[...]
    out_ref[...] = total.astype(BF16)


def call(kernel, out_shape, args, scratch=(), alias=None, flops=0):
    whole = pl.BlockSpec(memory_space=pltpu.VMEM)
    outs = jax.tree.map(lambda _: whole, out_shape)
    return pl.pallas_call(
        kernel,
        out_shape=jax.tree.map(lambda x: pltpu.VMEM(x.shape, x.dtype), out_shape),
        in_specs=[whole] * len(args),
        out_specs=outs,
        scratch_shapes=list(scratch),
        input_output_aliases=alias or {},
        compiler_params=pltpu.CompilerParams(vmem_limit_bytes=VMEM_LIMIT),
        cost_estimate=pl.CostEstimate(flops=flops, bytes_accessed=0, transcendentals=0),
    )(*args)


def per_device(features, kernel, grad_out):
    count, chan, slab, width = features.shape
    outs = kernel.shape[1]
    ring_size = lax.axis_size("cin")
    assert count == ring_size and grad_out.shape[0] == 1 and lax.axis_size("depth") == 2
    cells = slab * width
    half = ring_size // 2
    mid = outs // 2
    ring = ring_of(ring_size)
    fwd = [(ring[i], ring[(i + 1) % ring_size]) for i in range(ring_size)]
    bwd = [(j, i) for i, j in fwd]
    swap = [(0, 1), (1, 0)]
    token = jax.ShapeDtypeStruct((8, cells), F32)

    def send(pair):
        return lax.ppermute(pair[0], "cin", fwd), lax.ppermute(pair[1], "cin", bwd)

    grads = [None] * ring_size
    own = lax.optimization_barrier(grad_out.reshape(outs, cells))
    grads[0] = own
    going = send((own, own))

    feat = lax.optimization_barrier(features.transpose(0, 2, 1, 3))
    got = lax.ppermute(feat, "depth", swap)
    taps = kernel.transpose(0, 2, 1).reshape(3, 9 * chan, outs)
    w_out = call(turn_kernel, jax.ShapeDtypeStruct((3, outs, 9 * chan), BF16), (taps,))
    ext_shape = jax.ShapeDtypeStruct((count + 2, 3 * chan, cells + 2 * width), BF16)
    ext = call(functools.partial(extend_kernel, True), ext_shape, (feat, got))
    ext_other = call(functools.partial(extend_kernel, False), ext_shape, (got, feat))

    def forward(offsets, after=()):
        return call(
            functools.partial(forward_kernel, offsets, len(after), width),
            [jax.ShapeDtypeStruct((outs, cells), F32)] * len(offsets),
            (ext, w_out, *after),
        )

    def weight_all(mine, theirs, after):
        shape = (3, 9 * chan, outs)
        scale = 1.0 / math.sqrt(count * cells * lax.axis_size("depth"))
        whole = pl.BlockSpec(memory_space=pltpu.VMEM)
        args = (ext, ext_other, *mine, *theirs, after)
        return pl.pallas_call(
            functools.partial(weight_kernel, (near, far), width, scale),
            out_shape=[jax.ShapeDtypeStruct(shape, F32), token],
            in_specs=[whole] * len(args),
            out_specs=[pl.BlockSpec(memory_space=pl.ANY), whole],
            scratch_shapes=[pltpu.VMEM(shape, F32), pltpu.SemaphoreType.DMA((3,))],
            compiler_params=pltpu.CompilerParams(vmem_limit_bytes=VMEM_LIMIT),
            cost_estimate=pl.CostEstimate(flops=0, bytes_accessed=0, transcendentals=0),
        )(*args)

    parts = lax.axis_size("cout")

    def input_part(group, theirs, back, split):
        held = [grads[k] for k in group]
        first = back is None
        size = len(group)
        args = (taps, theirs, *held)
        whole = jax.ShapeDtypeStruct((count + 2, chan, cells), F32)
        kept = jax.ShapeDtypeStruct((count // 2, chan, cells), F32)
        pad = pltpu.VMEM((size, outs, cells + 2 * width), BF16)
        return call(
            functools.partial(input_kernel, group, first, count, split),
            [kept, kept] if split else [whole, token],
            args if first else (*args, back),
            scratch=[pltpu.VMEM(whole.shape, F32), pad] if split else [pad],
        )

    part = [None] * ring_size
    (part[half],) = forward([half])
    others = [k for k in range(ring_size) if k != half]
    near = [0, ring_size - 1, 1, ring_size - 2, 2]
    far = [k for k in range(ring_size) if k not in near]

    def slim(r):
        return r < half and 8 * r * r <= 9 * ring_size

    row = jax.ShapeDtypeStruct((outs, cells), BF16)
    back = None
    stacks = []
    tokens = []
    going = [[x] for x in going]
    sums = [[], []]
    for r in range(1, half + 1):
        rows_in = mid if r == half else outs
        rows_out = 0 if r == half else mid if r + 1 == half else outs
        sums_in = 0 if r == 1 else mid if r == 2 else outs
        sums_out = mid if r == 1 else outs
        unpack = r > 1 and slim(r - 1)
        packs = slim(r)
        raw = r <= 2 or not unpack
        apart = rows_out if r == 1 or not packs else 0
        group = near if r == 2 else far if r == half else []
        if r == 2:
            for k, p in zip(others, forward(others, [x for pair in sent_on for x in pair])):
                part[k] = p
        left = half + 1 - r
        late = tokens[-1][0:1] if tokens else 0.0
        kept, sent_on = [], []
        for i, perm in ((0, fwd), (1, bwd)):
            ins = going[i] if raw else []
            if unpack:
                ins = ins + [sums[i][0].astype(F32) + late]
            else:
                ins = ins + sums[i]
            shapes = [jax.ShapeDtypeStruct((apart, cells), BF16)] if apart else []
            if packs:
                packed_rows = rows_out - apart + sums_out + 16
                shapes = shapes + [jax.ShapeDtypeStruct((packed_rows, cells), F32)]
            else:
                shapes = shapes + [jax.ShapeDtypeStruct((sums_out, cells), F32)]
            sent = len(shapes)
            if rows_in and not raw:
                shapes = shapes + [jax.ShapeDtypeStruct((rows_in, cells), BF16)]
            plan = dict(
                back=bool(i),
                raw=raw,
                rows_in=rows_in,
                sums_in=sums_in,
                rows_out=rows_out,
                apart=apart,
                packs=packs,
                unpack=unpack,
                ins=len(ins),
                skip=len(tokens),
            )
            term = part[ring_size - left if i else left]
            relay = functools.partial(relay_kernel, plan)
            made = call(relay, shapes, (term, *ins, *tokens))
            kept.append(going[i][0] if raw else made[-1])
            total = made[sent - 1]
            sent_on.append([total])
            if packs:
                total = total.astype(jnp.float16)
            going[i] = [lax.ppermute(x, "cin", perm) for x in made[: sent - 1]]
            sums[i] = [lax.ppermute(total, "cin", perm)]
        if r == half:
            grads[half] = call(join_kernel, row, kept)
        else:
            grads[ring_size - r], grads[r] = kept
        tokens = []
        if group:
            size = len(group)
            stack = jax.ShapeDtypeStruct((size, outs, cells), BF16)
            mine = [grads[k] for k in group]
            mine = call(functools.partial(stack_kernel, size), stack, (*mine, *[x for pair in sent_on for x in pair]))
            theirs = lax.ppermute(mine, "depth", swap)
            back, token_i = input_part(group, theirs, back, r == half and parts == 2)
            stacks.append((mine, theirs))
            if r == half:
                kernel_grad, token_k = weight_all(*zip(*stacks), back)
            else:
                tokens = [token_i]
    (f,), (b,) = sums

    kernel_grad = kernel_grad.reshape(27, chan, outs).transpose(0, 2, 1)
    if parts == 2:
        terms = [back, lax.ppermute(token_i, "cout", swap)]
    else:
        back = back[1 : count + 1]
        terms = [lax.psum_scatter(back, "cout", scatter_dimension=0, tiled=True)]
    input_grad, token_i = call(
        functools.partial(add_kernel, len(terms)),
        [jax.ShapeDtypeStruct((count // parts, chan, cells), BF16), token],
        tuple(terms),
    )
    input_grad = input_grad.reshape(count // parts, chan, slab, width)
    output, _ = call(
        functools.partial(add_kernel, 3),
        [jax.ShapeDtypeStruct((outs, cells), BF16), token],
        (part[0], f, b, token_k),
    )
    output = output.reshape(1, outs, slab, width)
    return (output, input_grad, kernel_grad)


def solution(mesh):
    return jax.shard_map(
        per_device,
        mesh=mesh,
        in_specs=(
            P(None, "cin", "depth", None),
            P(None, "cout", "cin"),
            P("cin", "cout", "depth", None),
        ),
        out_specs=(
            P("cin", "cout", "depth", None),
            P("cout", "cin", "depth", None),
            P(None, "cout", "cin"),
        ),
        check_vma=False,
    )
```

```python
import functools
import math

import jax
import jax.numpy as jnp
from jax import lax
from jax.experimental import pallas as pl
from jax.experimental.pallas import tpu as pltpu
from jax.sharding import PartitionSpec as P

F32 = jnp.float32
BF16 = jnp.bfloat16
VMEM_LIMIT = 8 * 1024 * 1024


def ring_of(size):
    return list(range(0, size, 2)) + list(range(size - 1 - size % 2, 0, -2))


def shifted(x, by):
    width = x.shape[1]
    lane = lax.broadcasted_iota(jnp.int32, x.shape, 1)
    edge = 0 if by == 1 else width - 1
    return jnp.where(lane == edge, 0.0, pltpu.roll(x, by % width, 1))


def ring_row(k, size):
    me = lax.axis_index("cin")
    spot = jnp.where(me % 2 == 0, me // 2, size - 1 - me // 2)
    spot = (spot + k) % size
    return jnp.where(2 * spot < size + size % 2, 2 * spot, 2 * (size - 1 - spot) + 1)


def split_kernel(feat_ref, *outs):
    low = lax.axis_index("depth") == 0
    half = outs[0].shape[0]
    first, second = feat_ref[:, 0], feat_ref[:, 1]
    edge = jnp.where(low, second, first)
    outs[0][...] = edge[0:half]
    outs[1][...] = edge[half:]
    outs[2][...] = jnp.where(low, first, second)


def extend_kernel(own, feat_ref, edge_ref, second_edge_ref, *refs):
    ext_ref = refs[-1]
    count, slab, chan, width = feat_ref.shape
    half = edge_ref.shape[0]
    low = lax.axis_index("depth") == 0
    ext_ref[0] = jnp.zeros(ext_ref.shape[1:], BF16)
    ext_ref[count + 1] = jnp.zeros(ext_ref.shape[1:], BF16)
    for part, near_ref in enumerate((edge_ref, second_edge_ref)):

        @pl.loop(0, half)
        def _(i):
            h = part * half + i
            edge = near_ref[i]
            none = jnp.zeros_like(edge)
            first, second = feat_ref[h, 0], feat_ref[h, 1]
            if own:
                layers = [jnp.where(low, none, edge), first, second, jnp.where(low, edge, none)]
            else:
                rest = refs[0][h]
                layers = [jnp.where(low, second, none)]
                layers += [jnp.where(low, edge, rest), jnp.where(low, rest, edge)]
                layers += [jnp.where(low, none, first)]
            for d, x in enumerate(layers):
                wide = x.astype(F32)
                cols = slice(d * width, (d + 1) * width)
                ext_ref[h + 1, 0:chan, cols] = shifted(wide, 1).astype(BF16)
                ext_ref[h + 1, chan : 2 * chan, cols] = x
                ext_ref[h + 1, 2 * chan : 3 * chan, cols] = shifted(wide, -1).astype(BF16)


def turn_kernel(in_ref, out_ref):
    for a in range(in_ref.shape[0]):
        out_ref[a] = in_ref[a].T


def forward_kernel(offsets, skip, width, ext_ref, weight_ref, *part_refs):
    part_refs = part_refs[skip:]
    chan3 = ext_ref.shape[1]
    cells = ext_ref.shape[2] - 2 * width
    for k, part_ref in zip(offsets, part_refs):
        row = ring_row(k, ext_ref.shape[0] - 2)
        right = [
            ext_ref[pl.ds(row, 3), :, a * width : a * width + cells].reshape(3 * chan3, cells)
            for a in range(3)
        ]
        total = jnp.dot(
            jnp.concatenate([weight_ref[a] for a in range(3)], axis=1),
            jnp.concatenate(right, axis=0),
            preferred_element_type=F32,
        )
        part_ref[...] = total


def weight_kernel(group, width, scale, first, last, ext_ref, other_ref, mine_ref, theirs_ref, *refs):
    before = refs[:3]
    if not last:
        *outs, token_ref, second_token_ref = refs[-5:]
    else:
        out_ref, token_ref, second_token_ref, held_ref, sems = refs[-5:]
    second_token_ref[...] = jnp.zeros(second_token_ref.shape, F32)
    token_ref[...] = jnp.zeros(token_ref.shape, F32)
    chan3 = ext_ref.shape[1]
    cells = mine_ref.shape[2]
    terms = []
    for i, k in enumerate(group):
        row = ring_row(k, ext_ref.shape[0] - 2)
        terms.append((row, ext_ref, mine_ref, i))
        terms.append((row, other_ref, theirs_ref, i))
    copies = []
    for a in range(3):
        left = [
            source[pl.ds(row, 3), :, a * width : a * width + cells].reshape(3 * chan3, cells)
            for row, source, stack, i in terms
        ]
        total = lax.dot_general(
            jnp.concatenate(left, axis=1),
            jnp.concatenate([stack[i] for row, source, stack, i in terms], axis=1),
            (((1,), (1,)), ((), ())),
            preferred_element_type=F32,
        )
        if not first:
            total = before[a][...] + total
        if not last:
            outs[a][...] = total
            continue
        held_ref[a] = total * scale
        copies.append(pltpu.make_async_copy(held_ref.at[a], out_ref.at[a], sems.at[a]))
        copies[-1].start()
    for copy in copies:
        copy.wait()


def input_kernel(offsets, first, count, split, weight_ref, theirs_ref, *refs):
    size = len(offsets)
    grads = refs[:size]
    pad_ref = refs[-1]
    if split:
        mine_ref, sent_ref, acc_ref = refs[-4:-1]
    else:
        acc_ref, token_ref = refs[-3:-1]
        token_ref[...] = jnp.zeros(token_ref.shape, F32)
    chan, cells = acc_ref.shape[1:]
    width = (pad_ref.shape[2] - cells) // 2
    low = lax.axis_index("depth") == 0
    if first:
        acc_ref[...] = jnp.zeros(acc_ref.shape, F32)
    else:
        acc_ref[...] = refs[size][...]
    for i, (k, g_ref) in enumerate(zip(offsets, grads)):
        none = jnp.zeros((g_ref.shape[0], width), BF16)
        pad_ref[i, :, 0:width] = jnp.where(low, none, theirs_ref[i, :, cells - width :])
        pad_ref[i, :, width : width + cells] = g_ref[...]
        pad_ref[i, :, width + cells :] = jnp.where(low, theirs_ref[i, :, 0:width], none)
        for b in range(3):
            total = None
            for a in range(3):
                right = pad_ref[i, :, (2 - a) * width : (2 - a) * width + cells]
                left = weight_ref[a, 3 * b * chan : 3 * (b + 1) * chan]
                term = jnp.dot(left, right, preferred_element_type=F32)
                total = term if total is None else total + term
            row = ring_row(k, count) + b
            for d in range(cells // width):
                cols = slice(d * width, (d + 1) * width)
                acc_ref[row, :, cols] += (
                    shifted(total[0:chan, cols], -1)
                    + total[chan : 2 * chan, cols]
                    + shifted(total[2 * chan :, cols], 1)
                )
    if split:
        kept = count // 2
        side = lax.axis_index("cout")
        mine_ref[...] = acc_ref[pl.ds(1 + side * kept, kept)].reshape(kept * chan, cells)
        sent = acc_ref[pl.ds(1 + (1 - side) * kept, kept)].reshape(kept * chan, cells)
        sent_ref[kept * chan : kept * chan + 8] = jnp.zeros((8, cells), F32)
        coded(sent_ref, 0, kept * chan + 8, sent)


def power(k):
    whole = k.astype(jnp.int32)
    size = jnp.abs(whole)
    out = jnp.ones(k.shape, F32)
    for i in range(7):
        step = jnp.where(whole > 0, 2.0 ** (2**i), 2.0 ** -(2**i))
        out = out * jnp.where((size >> i) & 1 == 1, step, 1.0)
    return out


def packed(out_ref, at, spot, x):
    rows, cols = x.shape
    most = jnp.max(jnp.max(jnp.abs(x), axis=0, keepdims=True), axis=1, keepdims=True)
    most = jnp.broadcast_to(jnp.maximum(most, 2.0**-100), (8, cols))
    k = 13.0 - jnp.floor(jnp.log2(most))
    out_ref[at : at + rows] = x * power(k)[0:1]
    out_ref[spot : spot + 8] = k


def unpacked(ref, at, rows, spot):
    return ref[at : at + rows] * power(-ref[spot : spot + 8])[0:1]


EDGE = 2.0**-3.5


def coded(out_ref, at, spot, x):
    rows, cols = x.shape
    size = jnp.abs(x)
    most = jnp.max(jnp.max(size, axis=0, keepdims=True), axis=1, keepdims=True)
    most = jnp.broadcast_to(jnp.maximum(most, 2.0**-100), (8, cols))
    k = 2.0 - jnp.floor(jnp.log2(most))
    root = size * (power(k)[0:1] * 1.96) + EDGE
    square = root * root
    square = square * square
    out_ref[at : at + rows] = jnp.where(x < 0.0, -square, square)
    out_ref[spot : spot + 8] = k


def decoded(ref, at, rows, spot):
    value = ref[at : at + rows]
    size = jnp.abs(value)
    root = size * lax.rsqrt(size)
    root = root * lax.rsqrt(root) - EDGE
    root = root * (power(-ref[spot : spot + 8])[0:1] * (1.0 / 1.96))
    return jnp.where(value < 0.0, -root, root)


def relay_kernel(plan, part_ref, *refs):
    back, rows_in, sums_in, rows_out = (plan[n] for n in ("back", "rows_in", "sums_in", "rows_out"))
    ins, outs = list(refs[: plan["ins"]]), list(refs[plan["ins"] + plan["skip"] :])
    full = part_ref.shape[0]
    mid = full // 2
    came = total = None
    if plan["raw"]:
        came = ins.pop(0)[...]
    if plan["unpack"]:
        ref = ins.pop(0)
        spot = ref.shape[0] - 16
        held = 0 if plan["raw"] else rows_in
        if held:
            came = unpacked(ref, 0, held, spot).astype(BF16)
        total = decoded(ref, held, sums_in, spot + 8)
    elif sums_in:
        total = ins.pop(0)[...]
    if sums_in == 0:
        total = part_ref[mid:] if back else part_ref[0:mid]
    elif sums_in == mid:
        pair = [total, jnp.zeros_like(total)]
        total = part_ref[...] + jnp.concatenate(pair[::-1] if back else pair, axis=0)
    else:
        total = part_ref[...] + total
    if rows_out:
        passed = came[rows_in - rows_out :] if back else came[0:rows_out]
        if plan["apart"]:
            outs.pop(0)[...] = passed
            rows_out = 0
    if plan["packs"]:
        out_ref = outs.pop(0)
        spot = out_ref.shape[0] - 16
        if rows_out:
            packed(out_ref, 0, spot, passed.astype(F32))
        else:
            out_ref[spot : spot + 8] = jnp.zeros((8, out_ref.shape[1]), F32)
        coded(out_ref, rows_out, spot + 8, total)
    else:
        outs.pop(0)[...] = total
    if outs:
        outs.pop(0)[...] = came


def stack_kernel(count, *refs):
    out_ref = refs[-1]
    for i in range(count):
        out_ref[i] = refs[i][...]


def join_kernel(first_ref, second_ref, out_ref):
    mid = first_ref.shape[0]
    out_ref[0:mid] = first_ref[...]
    out_ref[mid:] = second_ref[...]


def add_kernel(first_ref, *refs, skip=0):
    out_ref, token_ref = refs[-2:]
    token_ref[...] = jnp.zeros(token_ref.shape, F32)
    total = first_ref[...]
    for ref in refs[: len(refs) - 2 - skip]:
        total = total + decoded(ref, 0, total.shape[0], total.shape[0] + 8)
    out_ref[...] = total.astype(BF16)


def call(kernel, out_shape, args, scratch=(), alias=None, flops=0):
    whole = pl.BlockSpec(memory_space=pltpu.VMEM)
    outs = jax.tree.map(lambda _: whole, out_shape)
    return pl.pallas_call(
        kernel,
        out_shape=jax.tree.map(lambda x: pltpu.VMEM(x.shape, x.dtype), out_shape),
        in_specs=[whole] * len(args),
        out_specs=outs,
        scratch_shapes=list(scratch),
        input_output_aliases=alias or {},
        compiler_params=pltpu.CompilerParams(vmem_limit_bytes=VMEM_LIMIT),
        cost_estimate=pl.CostEstimate(flops=flops, bytes_accessed=0, transcendentals=0),
    )(*args)


def per_device(features, kernel, grad_out):
    count, chan, slab, width = features.shape
    outs = kernel.shape[1]
    ring_size = lax.axis_size("cin")
    assert count == ring_size and slab == 2 and grad_out.shape[0] == 1 and lax.axis_size("depth") == 2
    cells = slab * width
    half = ring_size // 2
    mid = outs // 2
    ring = ring_of(ring_size)
    fwd = [(ring[i], ring[(i + 1) % ring_size]) for i in range(ring_size)]
    bwd = [(j, i) for i, j in fwd]
    swap = [(0, 1), (1, 0)]
    token = jax.ShapeDtypeStruct((8, cells), F32)

    def send(pair):
        return lax.ppermute(pair[0], "cin", fwd), lax.ppermute(pair[1], "cin", bwd)

    grads = [None] * ring_size
    own = lax.optimization_barrier(grad_out.reshape(outs, cells))
    grads[0] = own
    going = send((own, own))

    feat = features.transpose(0, 2, 1, 3)
    layer = [jax.ShapeDtypeStruct((n, chan, width), BF16) for n in (count // 2, count // 2, count)]
    got = [lax.ppermute(x, "depth", swap) for x in call(split_kernel, layer, (feat,))]
    taps = kernel.transpose(0, 2, 1).reshape(3, 9 * chan, outs)
    w_out = call(turn_kernel, jax.ShapeDtypeStruct((3, outs, 9 * chan), BF16), (taps,))
    ext_shape = jax.ShapeDtypeStruct((count + 2, 3 * chan, cells + 2 * width), BF16)
    ext = call(functools.partial(extend_kernel, True), ext_shape, (feat, *got[:2]))
    ext_other = call(functools.partial(extend_kernel, False), ext_shape, (feat, *got))

    def forward(offsets, after=()):
        return call(
            functools.partial(forward_kernel, offsets, len(after), width),
            [jax.ShapeDtypeStruct((outs, cells), F32)] * len(offsets),
            (ext, w_out, *after),
        )

    def weight_part(group, mine, theirs, acc, after):
        *acc, token_f, token_b = call(
            functools.partial(weight_kernel, group, width, 1.0, not acc, False),
            [jax.ShapeDtypeStruct((9 * chan, outs), F32)] * 3 + [token, token],
            (ext, ext_other, mine, theirs, *acc, after),
        )
        return acc, (token_f, token_b)

    def weight_last(group, mine, theirs, acc, after):
        shape = (3, 9 * chan, outs)
        scale = 1.0 / math.sqrt(count * cells * lax.axis_size("depth"))
        whole = pl.BlockSpec(memory_space=pltpu.VMEM)
        args = (ext, ext_other, mine, theirs, *acc, after)
        return pl.pallas_call(
            functools.partial(weight_kernel, group, width, scale, False, True),
            out_shape=[jax.ShapeDtypeStruct(shape, F32), token, token],
            in_specs=[whole] * len(args),
            out_specs=[pl.BlockSpec(memory_space=pl.ANY), whole, whole],
            scratch_shapes=[pltpu.VMEM(shape, F32), pltpu.SemaphoreType.DMA((3,))],
            compiler_params=pltpu.CompilerParams(vmem_limit_bytes=VMEM_LIMIT),
            cost_estimate=pl.CostEstimate(flops=0, bytes_accessed=0, transcendentals=0),
        )(*args)

    parts = lax.axis_size("cout")

    def input_part(group, theirs, back, split):
        held = [grads[k] for k in group]
        first = back is None
        size = len(group)
        args = (taps, theirs, *held)
        whole = jax.ShapeDtypeStruct((count + 2, chan, cells), F32)
        kept = jax.ShapeDtypeStruct((count // 2 * chan, cells), F32)
        sent = jax.ShapeDtypeStruct((count // 2 * chan + 16, cells), F32)
        pad = pltpu.VMEM((size, outs, cells + 2 * width), BF16)
        return call(
            functools.partial(input_kernel, group, first, count, split),
            [kept, sent] if split else [whole, token],
            args if first else (*args, back),
            scratch=[pltpu.VMEM(whole.shape, F32), pad] if split else [pad],
        )

    part = [None] * ring_size
    (part[half],) = forward([half])
    others = [k for k in range(ring_size) if k != half]
    near = [0, ring_size - 1, 1, ring_size - 2, 2]
    far = [k for k in range(ring_size) if k not in near]

    row = jax.ShapeDtypeStruct((outs, cells), BF16)
    back = None
    acc = []
    tokens = []
    going = [[x] for x in going]
    sums = [[], []]
    for r in range(1, half + 1):
        rows_in = mid if r == half else outs
        rows_out = 0 if r == half else mid if r + 1 == half else outs
        sums_in = 0 if r == 1 else mid if r == 2 else outs
        sums_out = mid if r == 1 else outs
        unpack = r > 1
        packs = True
        raw = r <= 2 or not unpack
        apart = rows_out if r == 1 or not packs else 0
        group = near if r == 2 else far if r == half else []
        if r == 2:
            for k, p in zip(others, forward(others, [x for pair in sent_on for x in pair])):
                part[k] = p
        left = half + 1 - r
        kept, sent_on = [], []
        for i, perm in ((0, fwd), (1, bwd)):
            ins = going[i] if raw else []
            if unpack:
                late = tokens[i][0:1] if tokens else 0.0
                ins = ins + [sums[i][0].astype(F32) + late]
            else:
                ins = ins + sums[i]
            shapes = [jax.ShapeDtypeStruct((apart, cells), BF16)] if apart else []
            if packs:
                packed_rows = rows_out - apart + sums_out + 16
                shapes = shapes + [jax.ShapeDtypeStruct((packed_rows, cells), F32)]
            else:
                shapes = shapes + [jax.ShapeDtypeStruct((sums_out, cells), F32)]
            sent = len(shapes)
            if rows_in and not raw:
                shapes = shapes + [jax.ShapeDtypeStruct((rows_in, cells), BF16)]
            plan = dict(
                back=bool(i),
                raw=raw,
                rows_in=rows_in,
                sums_in=sums_in,
                rows_out=rows_out,
                apart=apart,
                packs=packs,
                unpack=unpack,
                ins=len(ins),
                skip=0,
            )
            term = part[ring_size - left if i else left]
            relay = functools.partial(relay_kernel, plan)
            made = call(relay, shapes, (term, *ins))
            kept.append(going[i][0] if raw else made[-1])
            total = made[sent - 1]
            sent_on.append([total])
            if packs:
                total = total.astype(jnp.float16)
            going[i] = [lax.ppermute(x, "cin", perm) for x in made[: sent - 1]]
            sums[i] = [lax.ppermute(total, "cin", perm)]
        if r == half:
            grads[half] = call(join_kernel, row, kept)
        else:
            grads[ring_size - r], grads[r] = kept
        tokens = []
        if group:
            size = len(group)
            stack = jax.ShapeDtypeStruct((size, outs, cells), BF16)
            mine = [grads[k] for k in group]
            mine = call(functools.partial(stack_kernel, size), stack, (*mine, *[x for pair in sent_on for x in pair]))
            theirs = lax.ppermute(mine, "depth", swap)
            back, token_i = input_part(group, theirs, back, r == half and parts == 2)
            if r == half:
                kernel_grad, *tokens = weight_last(group, mine, theirs, acc, back)
            else:
                acc, tokens = weight_part(group, mine, theirs, acc, token_i)
    (f,), (b,) = sums

    kernel_grad = kernel_grad.reshape(27, chan, outs).transpose(0, 2, 1)
    if parts == 2:
        other = lax.ppermute(token_i.astype(jnp.float16), "cout", swap).astype(F32)
        terms = [back, other]
    else:
        back = back[1 : count + 1]
        terms = [lax.psum_scatter(back, "cout", scatter_dimension=0, tiled=True)]
        terms = [terms[0].reshape(count // parts * chan, cells)]
    input_grad, token_y = call(
        add_kernel,
        [jax.ShapeDtypeStruct((count // parts * chan, cells), BF16), token],
        tuple(terms),
    )
    input_grad = input_grad.reshape(count // parts, chan, slab, width)
    output, _ = call(
        functools.partial(add_kernel, skip=1),
        [jax.ShapeDtypeStruct((outs, cells), BF16), token],
        (part[0], f.astype(F32), b.astype(F32), token_y),
    )
    output = output.reshape(1, outs, slab, width)
    return (output, input_grad, kernel_grad)


def solution(mesh):
    return jax.shard_map(
        per_device,
        mesh=mesh,
        in_specs=(
            P(None, "cin", "depth", None),
            P(None, "cout", "cin"),
            P("cin", "cout", "depth", None),
        ),
        out_specs=(
            P("cin", "cout", "depth", None),
            P("cout", "cin", "depth", None),
            P(None, "cout", "cin"),
        ),
        check_vma=False,
    )
```

```python
import functools
import math

import jax
import jax.numpy as jnp
from jax import lax
from jax.experimental import pallas as pl
from jax.experimental.pallas import tpu as pltpu
from jax.sharding import PartitionSpec as P

F32 = jnp.float32
BF16 = jnp.bfloat16
VMEM_LIMIT = 8 * 1024 * 1024


def ring_of(size):
    return list(range(0, size, 2)) + list(range(size - 1 - size % 2, 0, -2))


def shifted(x, by):
    width = x.shape[1]
    lane = lax.broadcasted_iota(jnp.int32, x.shape, 1)
    edge = 0 if by == 1 else width - 1
    return jnp.where(lane == edge, 0.0, pltpu.roll(x, by % width, 1))


def ring_row(k, size):
    me = lax.axis_index("cin")
    spot = jnp.where(me % 2 == 0, me // 2, size - 1 - me // 2)
    spot = (spot + k) % size
    return jnp.where(2 * spot < size + size % 2, 2 * spot, 2 * (size - 1 - spot) + 1)


def split_kernel(feat_ref, *outs):
    low = lax.axis_index("depth") == 0
    half = outs[0].shape[0]
    first, second = feat_ref[:, 0], feat_ref[:, 1]
    edge = jnp.where(low, second, first)
    outs[0][...] = edge[0:half]
    outs[1][...] = edge[half:]
    outs[2][...] = jnp.where(low, first, second)


def extend_kernel(own, feat_ref, edge_ref, second_edge_ref, *refs):
    ext_ref = refs[-1]
    count, slab, chan, width = feat_ref.shape
    half = edge_ref.shape[0]
    low = lax.axis_index("depth") == 0
    ext_ref[0] = jnp.zeros(ext_ref.shape[1:], BF16)
    ext_ref[count + 1] = jnp.zeros(ext_ref.shape[1:], BF16)
    for part, near_ref in enumerate((edge_ref, second_edge_ref)):

        @pl.loop(0, half)
        def _(i):
            h = part * half + i
            edge = near_ref[i]
            none = jnp.zeros_like(edge)
            first, second = feat_ref[h, 0], feat_ref[h, 1]
            if own:
                layers = [jnp.where(low, none, edge), first, second, jnp.where(low, edge, none)]
            else:
                rest = refs[0][h]
                layers = [jnp.where(low, second, none)]
                layers += [jnp.where(low, edge, rest), jnp.where(low, rest, edge)]
                layers += [jnp.where(low, none, first)]
            for d, x in enumerate(layers):
                wide = x.astype(F32)
                cols = slice(d * width, (d + 1) * width)
                ext_ref[h + 1, 0:chan, cols] = shifted(wide, 1).astype(BF16)
                ext_ref[h + 1, chan : 2 * chan, cols] = x
                ext_ref[h + 1, 2 * chan : 3 * chan, cols] = shifted(wide, -1).astype(BF16)


def turn_kernel(in_ref, after_ref, out_ref):
    for a in range(in_ref.shape[0]):
        out_ref[a] = in_ref[a].T


def forward_kernel(offsets, skip, width, ext_ref, weight_ref, *part_refs):
    part_refs = part_refs[skip:]
    chan3 = ext_ref.shape[1]
    cells = ext_ref.shape[2] - 2 * width
    for k, part_ref in zip(offsets, part_refs):
        row = ring_row(k, ext_ref.shape[0] - 2)
        right = [
            ext_ref[pl.ds(row, 3), :, a * width : a * width + cells].reshape(3 * chan3, cells)
            for a in range(3)
        ]
        total = jnp.dot(
            jnp.concatenate([weight_ref[a] for a in range(3)], axis=1),
            jnp.concatenate(right, axis=0),
            preferred_element_type=F32,
        )
        part_ref[...] = total


def weight_kernel(group, width, scale, first, last, depths, ext_ref, other_ref, mine_ref, theirs_ref, *refs):
    before = refs[:3]
    if not last:
        *outs, token_ref, second_token_ref = refs[-5:]
        second_token_ref[...] = jnp.zeros(second_token_ref.shape, F32)
        token_ref[...] = jnp.zeros(token_ref.shape, F32)
    else:
        out_ref, held_ref, sems = refs[-3:]
    chan3 = ext_ref.shape[1]
    cells = mine_ref.shape[2]
    terms = []
    for i, k in enumerate(group):
        row = ring_row(k, ext_ref.shape[0] - 2)
        terms.append((row, ext_ref, mine_ref, i))
        terms.append((row, other_ref, theirs_ref, i))
    copies = []
    for a in depths:
        left = [
            source[pl.ds(row, 3), :, a * width : a * width + cells].reshape(3 * chan3, cells)
            for row, source, stack, i in terms
        ]
        total = lax.dot_general(
            jnp.concatenate(left, axis=1),
            jnp.concatenate([stack[i] for row, source, stack, i in terms], axis=1),
            (((1,), (1,)), ((), ())),
            preferred_element_type=F32,
        )
        if not first:
            total = before[a][...] + total
        if not last:
            outs[a][...] = total
            continue
        slot = len(copies)
        held_ref[slot] = total * scale
        copy = pltpu.make_async_copy(held_ref.at[slot], out_ref.at[a], sems.at[slot])
        copies.append(copy)
        copies[-1].start()
    for copy in copies:
        copy.wait()


def input_kernel(offsets, first, count, split, weight_ref, theirs_ref, *refs):
    size = len(offsets)
    grads = refs[:size]
    pad_ref = refs[-1]
    if split:
        mine_ref, sent_ref, acc_ref = refs[-4:-1]
    else:
        acc_ref, token_ref = refs[-3:-1]
        token_ref[...] = jnp.zeros(token_ref.shape, F32)
    chan, cells = acc_ref.shape[1:]
    width = (pad_ref.shape[2] - cells) // 2
    low = lax.axis_index("depth") == 0
    if first:
        acc_ref[...] = jnp.zeros(acc_ref.shape, F32)
    else:
        acc_ref[...] = refs[size][...]
    for i, (k, g_ref) in enumerate(zip(offsets, grads)):
        none = jnp.zeros((g_ref.shape[0], width), BF16)
        pad_ref[i, :, 0:width] = jnp.where(low, none, theirs_ref[i, :, cells - width :])
        pad_ref[i, :, width : width + cells] = g_ref[...]
        pad_ref[i, :, width + cells :] = jnp.where(low, theirs_ref[i, :, 0:width], none)
        for b in range(3):
            total = None
            for a in range(3):
                right = pad_ref[i, :, (2 - a) * width : (2 - a) * width + cells]
                left = weight_ref[a, 3 * b * chan : 3 * (b + 1) * chan]
                term = jnp.dot(left, right, preferred_element_type=F32)
                total = term if total is None else total + term
            row = ring_row(k, count) + b
            for d in range(cells // width):
                cols = slice(d * width, (d + 1) * width)
                acc_ref[row, :, cols] += (
                    shifted(total[0:chan, cols], -1)
                    + total[chan : 2 * chan, cols]
                    + shifted(total[2 * chan :, cols], 1)
                )
    if split:
        kept = count // 2
        side = lax.axis_index("cout")
        mine_ref[...] = acc_ref[pl.ds(1 + side * kept, kept)].reshape(kept * chan, cells)
        sent = acc_ref[pl.ds(1 + (1 - side) * kept, kept)].reshape(kept * chan, cells)
        sent_ref[kept * chan : kept * chan + 8] = jnp.zeros((8, cells), F32)
        coded(sent_ref, 0, kept * chan + 8, sent)


def power(k):
    whole = k.astype(jnp.int32)
    size = jnp.abs(whole)
    out = jnp.ones(k.shape, F32)
    for i in range(7):
        step = jnp.where(whole > 0, 2.0 ** (2**i), 2.0 ** -(2**i))
        out = out * jnp.where((size >> i) & 1 == 1, step, 1.0)
    return out


def packed(out_ref, at, spot, x):
    rows, cols = x.shape
    most = jnp.max(jnp.max(jnp.abs(x), axis=0, keepdims=True), axis=1, keepdims=True)
    most = jnp.broadcast_to(jnp.maximum(most, 2.0**-100), (8, cols))
    k = 13.0 - jnp.floor(jnp.log2(most))
    out_ref[at : at + rows] = x * power(k)[0:1]
    out_ref[spot : spot + 8] = k


def unpacked(ref, at, rows, spot):
    return ref[at : at + rows] * power(-ref[spot : spot + 8])[0:1]


EDGE = 2.0**-3.5


def coded(out_ref, at, spot, x):
    rows, cols = x.shape
    size = jnp.abs(x)
    most = jnp.max(jnp.max(size, axis=0, keepdims=True), axis=1, keepdims=True)
    most = jnp.broadcast_to(jnp.maximum(most, 2.0**-100), (8, cols))
    k = 2.0 - jnp.floor(jnp.log2(most))
    root = size * (power(k)[0:1] * 1.96) + EDGE
    square = root * root
    square = square * square
    out_ref[at : at + rows] = jnp.where(x < 0.0, -square, square)
    out_ref[spot : spot + 8] = k


def decoded(ref, at, rows, spot):
    value = ref[at : at + rows]
    size = jnp.abs(value)
    root = size * lax.rsqrt(size)
    root = root * lax.rsqrt(root) - EDGE
    root = root * (power(-ref[spot : spot + 8])[0:1] * (1.0 / 1.96))
    return jnp.where(value < 0.0, -root, root)


def relay_kernel(plan, part_ref, *refs):
    back, rows_in, sums_in, rows_out = (plan[n] for n in ("back", "rows_in", "sums_in", "rows_out"))
    ins, outs = list(refs[: plan["ins"]]), list(refs[plan["ins"] + plan["skip"] :])
    full = part_ref.shape[0]
    mid = full // 2
    came = total = None
    if plan["raw"]:
        came = ins.pop(0)[...]
    if plan["unpack"]:
        ref = ins.pop(0)
        spot = ref.shape[0] - 16
        held = 0 if plan["raw"] else rows_in
        if held:
            came = unpacked(ref, 0, held, spot).astype(BF16)
        total = decoded(ref, held, sums_in, spot + 8)
    elif sums_in:
        total = ins.pop(0)[...]
    if sums_in == 0:
        total = part_ref[mid:] if back else part_ref[0:mid]
    elif sums_in == mid:
        pair = [total, jnp.zeros_like(total)]
        total = part_ref[...] + jnp.concatenate(pair[::-1] if back else pair, axis=0)
    else:
        total = part_ref[...] + total
    if rows_out:
        passed = came[rows_in - rows_out :] if back else came[0:rows_out]
        if plan["apart"]:
            outs.pop(0)[...] = passed
            rows_out = 0
    if plan["packs"]:
        out_ref = outs.pop(0)
        spot = out_ref.shape[0] - 16
        if rows_out:
            packed(out_ref, 0, spot, passed.astype(F32))
        else:
            out_ref[spot : spot + 8] = jnp.zeros((8, out_ref.shape[1]), F32)
        coded(out_ref, rows_out, spot + 8, total)
    else:
        outs.pop(0)[...] = total
    if outs:
        outs.pop(0)[...] = came


def mark_kernel(after_ref, token_ref, second_token_ref):
    token_ref[...] = jnp.zeros(token_ref.shape, F32)
    second_token_ref[...] = jnp.zeros(second_token_ref.shape, F32)


def stack_kernel(count, *refs):
    out_ref = refs[-1]
    for i in range(count):
        out_ref[i] = refs[i][...]


def join_kernel(first_ref, second_ref, out_ref):
    mid = first_ref.shape[0]
    out_ref[0:mid] = first_ref[...]
    out_ref[mid:] = second_ref[...]


def add_kernel(first_ref, *refs, skip=0):
    out_ref = refs[-1]
    total = first_ref[...]
    for ref in refs[: len(refs) - 1 - skip]:
        total = total + decoded(ref, 0, total.shape[0], total.shape[0] + 8)
    out_ref[...] = total.astype(BF16)


def call(kernel, out_shape, args, scratch=(), alias=None, flops=0):
    whole = pl.BlockSpec(memory_space=pltpu.VMEM)
    outs = jax.tree.map(lambda _: whole, out_shape)
    return pl.pallas_call(
        kernel,
        out_shape=jax.tree.map(lambda x: pltpu.VMEM(x.shape, x.dtype), out_shape),
        in_specs=[whole] * len(args),
        out_specs=outs,
        scratch_shapes=list(scratch),
        input_output_aliases=alias or {},
        compiler_params=pltpu.CompilerParams(vmem_limit_bytes=VMEM_LIMIT),
        cost_estimate=pl.CostEstimate(flops=flops, bytes_accessed=0, transcendentals=0),
    )(*args)


def per_device(features, kernel, grad_out):
    count, chan, slab, width = features.shape
    outs = kernel.shape[1]
    ring_size = lax.axis_size("cin")
    assert count == ring_size and slab == 2 and grad_out.shape[0] == 1 and lax.axis_size("depth") == 2
    cells = slab * width
    half = ring_size // 2
    mid = outs // 2
    ring = ring_of(ring_size)
    fwd = [(ring[i], ring[(i + 1) % ring_size]) for i in range(ring_size)]
    bwd = [(j, i) for i, j in fwd]
    swap = [(0, 1), (1, 0)]
    token = jax.ShapeDtypeStruct((8, cells), F32)

    def send(pair):
        return lax.ppermute(pair[0], "cin", fwd), lax.ppermute(pair[1], "cin", bwd)

    grads = [None] * ring_size
    own = lax.optimization_barrier(grad_out.reshape(outs, cells))
    grads[0] = own
    going = send((own, own))

    feat = features.transpose(0, 2, 1, 3)
    layer = [jax.ShapeDtypeStruct((n, chan, width), BF16) for n in (count // 2, count // 2, count)]
    got = [lax.ppermute(x, "depth", swap) for x in call(split_kernel, layer, (feat,))]
    taps = kernel.transpose(0, 2, 1).reshape(3, 9 * chan, outs)
    ext_shape = jax.ShapeDtypeStruct((count + 2, 3 * chan, cells + 2 * width), BF16)
    ext = call(functools.partial(extend_kernel, True), ext_shape, (feat, *got[:2]))
    w_out = call(turn_kernel, jax.ShapeDtypeStruct((3, outs, 9 * chan), BF16), (taps, ext))
    ext_other = call(functools.partial(extend_kernel, False), ext_shape, (feat, *got))

    def forward(offsets, after=()):
        return call(
            functools.partial(forward_kernel, offsets, len(after), width),
            [jax.ShapeDtypeStruct((outs, cells), F32)] * len(offsets),
            (ext, w_out, *after),
        )

    def weight_part(group, mine, theirs, acc, after):
        *acc, token_f, token_b = call(
            functools.partial(weight_kernel, group, width, 1.0, not acc, False, range(3)),
            [jax.ShapeDtypeStruct((9 * chan, outs), F32)] * 3 + [token, token],
            (ext, ext_other, mine, theirs, *acc, after),
        )
        return acc, (token_f, token_b)

    def weight_last(group, mine, theirs, acc, after, depths, made):
        shape = (3, 9 * chan, outs)
        scale = 1.0 / math.sqrt(count * cells * lax.axis_size("depth"))
        whole = pl.BlockSpec(memory_space=pltpu.VMEM)
        anywhere = pl.BlockSpec(memory_space=pl.ANY)
        args = (ext, ext_other, mine, theirs, *acc, after, *made)
        size = len(depths)
        return pl.pallas_call(
            functools.partial(weight_kernel, group, width, scale, False, True, depths),
            out_shape=jax.ShapeDtypeStruct(shape, F32),
            in_specs=[whole] * (len(args) - len(made)) + [anywhere] * len(made),
            out_specs=anywhere,
            scratch_shapes=[pltpu.VMEM((size, *shape[1:]), F32), pltpu.SemaphoreType.DMA((size,))],
            input_output_aliases={len(args) - 1: 0} if made else {},
            compiler_params=pltpu.CompilerParams(vmem_limit_bytes=VMEM_LIMIT),
            cost_estimate=pl.CostEstimate(flops=0, bytes_accessed=0, transcendentals=0),
        )(*args)

    parts = lax.axis_size("cout")

    def input_part(group, theirs, back, split):
        held = [grads[k] for k in group]
        first = back is None
        size = len(group)
        args = (taps, theirs, *held)
        whole = jax.ShapeDtypeStruct((count + 2, chan, cells), F32)
        kept = jax.ShapeDtypeStruct((count // 2 * chan, cells), F32)
        sent = jax.ShapeDtypeStruct((count // 2 * chan + 16, cells), F32)
        pad = pltpu.VMEM((size, outs, cells + 2 * width), BF16)
        return call(
            functools.partial(input_kernel, group, first, count, split),
            [kept, sent] if split else [whole, token],
            args if first else (*args, back),
            scratch=[pltpu.VMEM(whole.shape, F32), pad] if split else [pad],
        )

    part = [None] * ring_size
    (part[half],) = forward([half])
    others = [k for k in range(ring_size) if k != half]
    near = [0, ring_size - 1, 1, ring_size - 2, 2]
    far = [k for k in range(ring_size) if k not in near]

    row = jax.ShapeDtypeStruct((outs, cells), BF16)
    back = None
    acc = []
    tokens = []
    going = [[x] for x in going]
    sums = [[], []]
    for r in range(1, half + 1):
        rows_in = mid if r == half else outs
        rows_out = 0 if r == half else mid if r + 1 == half else outs
        sums_in = 0 if r == 1 else mid if r == 2 else outs
        sums_out = mid if r == 1 else outs
        unpack = r > 1
        packs = True
        raw = r <= 2 or not unpack
        apart = rows_out if r == 1 or not packs else 0
        group = near if r == 2 else far if r == half else []
        if r == 2:
            for k, p in zip(others, forward(others, [x for pair in sent_on for x in pair])):
                part[k] = p
        left = half + 1 - r
        kept, sent_on = [], []
        for i, perm in ((0, fwd), (1, bwd)):
            ins = going[i] if raw else []
            if unpack:
                late = tokens[i][0:1] if tokens else 0.0
                ins = ins + [sums[i][0].astype(F32) + late]
            else:
                ins = ins + sums[i]
            shapes = [jax.ShapeDtypeStruct((apart, cells), BF16)] if apart else []
            if packs:
                packed_rows = rows_out - apart + sums_out + 16
                shapes = shapes + [jax.ShapeDtypeStruct((packed_rows, cells), F32)]
            else:
                shapes = shapes + [jax.ShapeDtypeStruct((sums_out, cells), F32)]
            sent = len(shapes)
            if rows_in and not raw:
                shapes = shapes + [jax.ShapeDtypeStruct((rows_in, cells), BF16)]
            plan = dict(
                back=bool(i),
                raw=raw,
                rows_in=rows_in,
                sums_in=sums_in,
                rows_out=rows_out,
                apart=apart,
                packs=packs,
                unpack=unpack,
                ins=len(ins),
                skip=0,
            )
            term = part[ring_size - left if i else left]
            relay = functools.partial(relay_kernel, plan)
            made = call(relay, shapes, (term, *ins))
            kept.append(going[i][0] if raw else made[-1])
            total = made[sent - 1]
            sent_on.append([total])
            if packs:
                total = total.astype(jnp.float16)
            going[i] = [lax.ppermute(x, "cin", perm) for x in made[: sent - 1]]
            sums[i] = [lax.ppermute(total, "cin", perm)]
        if r == half:
            grads[half] = call(join_kernel, row, kept)
        else:
            grads[ring_size - r], grads[r] = kept
        tokens = []
        if group:
            size = len(group)
            stack = jax.ShapeDtypeStruct((size, outs, cells), BF16)
            mine = [grads[k] for k in group]
            mine = call(functools.partial(stack_kernel, size), stack, (*mine, *[x for pair in sent_on for x in pair]))
            theirs = lax.ppermute(mine, "depth", swap)
            back, token_i = input_part(group, theirs, back, r == half and parts == 2)
            if r == half:
                tokens = call(mark_kernel, [token, token], (back,))
                kernel_grad = weight_last(group, mine, theirs, acc, tokens[0], range(3), ())
            else:
                acc, tokens = weight_part(group, mine, theirs, acc, token_i)
    (f,), (b,) = sums

    kernel_grad = kernel_grad.reshape(27, chan, outs).transpose(0, 2, 1)
    if parts == 2:
        other = lax.ppermute(token_i.astype(jnp.float16), "cout", swap).astype(F32)
        terms = [back, other]
    else:
        back = back[1 : count + 1]
        terms = [lax.psum_scatter(back, "cout", scatter_dimension=0, tiled=True)]
        terms = [terms[0].reshape(count // parts * chan, cells)]
    input_grad = call(
        add_kernel,
        jax.ShapeDtypeStruct((count // parts * chan, cells), BF16),
        tuple(terms),
    )
    input_grad = input_grad.reshape(count // parts, chan, slab, width)
    output = call(
        functools.partial(add_kernel, skip=1),
        jax.ShapeDtypeStruct((outs, cells), BF16),
        (part[0], f.astype(F32) + tokens[0][0:1], b.astype(F32) + tokens[1][0:1], input_grad),
    )
    output = output.reshape(1, outs, slab, width)
    return (output, input_grad, kernel_grad)


def solution(mesh):
    return jax.shard_map(
        per_device,
        mesh=mesh,
        in_specs=(
            P(None, "cin", "depth", None),
            P(None, "cout", "cin"),
            P("cin", "cout", "depth", None),
        ),
        out_specs=(
            P("cin", "cout", "depth", None),
            P("cout", "cin", "depth", None),
            P(None, "cout", "cin"),
        ),
        check_vma=False,
    )
```

```python
import functools
import math

import jax
import jax.numpy as jnp
from jax import lax
from jax.experimental import pallas as pl
from jax.experimental.pallas import tpu as pltpu
from jax.sharding import PartitionSpec as P

F32 = jnp.float32
BF16 = jnp.bfloat16
VMEM_LIMIT = 8 * 1024 * 1024


def ring_of(size):
    return list(range(0, size, 2)) + list(range(size - 1 - size % 2, 0, -2))


def shifted(x, by):
    width = x.shape[1]
    lane = lax.broadcasted_iota(jnp.int32, x.shape, 1)
    edge = 0 if by == 1 else width - 1
    return jnp.where(lane == edge, 0.0, pltpu.roll(x, by % width, 1))


def ring_row(k, size):
    me = lax.axis_index("cin")
    spot = jnp.where(me % 2 == 0, me // 2, size - 1 - me // 2)
    spot = (spot + k) % size
    return jnp.where(2 * spot < size + size % 2, 2 * spot, 2 * (size - 1 - spot) + 1)


def split_kernel(feat_ref, *outs):
    low = lax.axis_index("depth") == 0
    half = outs[0].shape[0]
    first, second = feat_ref[:, 0], feat_ref[:, 1]
    edge = jnp.where(low, second, first)
    outs[0][...] = edge[0:half]
    outs[1][...] = edge[half:]
    outs[2][...] = jnp.where(low, first, second)


def extend_kernel(own, feat_ref, edge_ref, second_edge_ref, *refs):
    ext_ref = refs[-1]
    count, slab, chan, width = feat_ref.shape
    half = edge_ref.shape[0]
    low = lax.axis_index("depth") == 0
    ext_ref[0] = jnp.zeros(ext_ref.shape[1:], BF16)
    ext_ref[count + 1] = jnp.zeros(ext_ref.shape[1:], BF16)
    for part, near_ref in enumerate((edge_ref, second_edge_ref)):

        @pl.loop(0, half)
        def _(i):
            h = part * half + i
            edge = near_ref[i]
            none = jnp.zeros_like(edge)
            first, second = feat_ref[h, 0], feat_ref[h, 1]
            if own:
                layers = [jnp.where(low, none, edge), first, second, jnp.where(low, edge, none)]
            else:
                rest = refs[0][h]
                layers = [jnp.where(low, second, none)]
                layers += [jnp.where(low, edge, rest), jnp.where(low, rest, edge)]
                layers += [jnp.where(low, none, first)]
            for d, x in enumerate(layers):
                wide = x.astype(F32)
                cols = slice(d * width, (d + 1) * width)
                ext_ref[h + 1, 0:chan, cols] = shifted(wide, 1).astype(BF16)
                ext_ref[h + 1, chan : 2 * chan, cols] = x
                ext_ref[h + 1, 2 * chan : 3 * chan, cols] = shifted(wide, -1).astype(BF16)


def turn_kernel(in_ref, after_ref, out_ref):
    for a in range(in_ref.shape[0]):
        out_ref[a] = in_ref[a].T


def forward_kernel(offsets, skip, width, ext_ref, weight_ref, *part_refs):
    part_refs = part_refs[skip:]
    chan3 = ext_ref.shape[1]
    cells = ext_ref.shape[2] - 2 * width
    for k, part_ref in zip(offsets, part_refs):
        row = ring_row(k, ext_ref.shape[0] - 2)
        right = [
            ext_ref[pl.ds(row, 3), :, a * width : a * width + cells].reshape(3 * chan3, cells)
            for a in range(3)
        ]
        total = jnp.dot(
            jnp.concatenate([weight_ref[a] for a in range(3)], axis=1),
            jnp.concatenate(right, axis=0),
            preferred_element_type=F32,
        )
        part_ref[...] = total


def weight_kernel(group, width, scale, first, last, depths, ext_ref, other_ref, mine_ref, theirs_ref, *refs):
    before = refs[:3]
    if not last:
        *outs, token_ref, second_token_ref = refs[-5:]
        second_token_ref[...] = jnp.zeros(second_token_ref.shape, F32)
        token_ref[...] = jnp.zeros(token_ref.shape, F32)
    else:
        out_ref, held_ref, sems = refs[-3:]
    chan3 = ext_ref.shape[1]
    cells = mine_ref.shape[2]
    terms = []
    for i, k in enumerate(group):
        row = ring_row(k, ext_ref.shape[0] - 2)
        terms.append((row, ext_ref, mine_ref, i))
        terms.append((row, other_ref, theirs_ref, i))
    copies = []
    for a in depths:
        left = [
            source[pl.ds(row, 3), :, a * width : a * width + cells].reshape(3 * chan3, cells)
            for row, source, stack, i in terms
        ]
        total = lax.dot_general(
            jnp.concatenate(left, axis=1),
            jnp.concatenate([stack[i] for row, source, stack, i in terms], axis=1),
            (((1,), (1,)), ((), ())),
            preferred_element_type=F32,
        )
        if not first:
            total = before[a][...] + total
        if not last:
            outs[a][...] = total
            continue
        slot = len(copies)
        held_ref[slot] = total * scale
        copy = pltpu.make_async_copy(held_ref.at[slot], out_ref.at[a], sems.at[slot])
        copies.append(copy)
        copies[-1].start()
    for copy in copies:
        copy.wait()


def input_kernel(offsets, first, count, split, weight_ref, theirs_ref, *refs):
    size = len(offsets)
    grads = refs[:size]
    pad_ref = refs[-1]
    if split:
        mine_ref, sent_ref, acc_ref = refs[-4:-1]
    else:
        acc_ref, token_ref = refs[-3:-1]
        token_ref[...] = jnp.zeros(token_ref.shape, F32)
    chan, cells = acc_ref.shape[1:]
    width = (pad_ref.shape[2] - cells) // 2
    low = lax.axis_index("depth") == 0
    if first:
        acc_ref[...] = jnp.zeros(acc_ref.shape, F32)
    else:
        acc_ref[...] = refs[size][...]
    for i, (k, g_ref) in enumerate(zip(offsets, grads)):
        none = jnp.zeros((g_ref.shape[0], width), BF16)
        pad_ref[i, :, 0:width] = jnp.where(low, none, theirs_ref[i, :, cells - width :])
        pad_ref[i, :, width : width + cells] = g_ref[...]
        pad_ref[i, :, width + cells :] = jnp.where(low, theirs_ref[i, :, 0:width], none)
        right = [
            pad_ref[i, :, (2 - a) * width : (2 - a) * width + cells] for a in range(3)
        ]
        right = jnp.concatenate(right, axis=0)
        for b in range(3):
            left = [weight_ref[a, 3 * b * chan : 3 * (b + 1) * chan] for a in range(3)]
            total = jnp.dot(
                jnp.concatenate(left, axis=1), right, preferred_element_type=F32
            )
            row = ring_row(k, count) + b
            for d in range(cells // width):
                cols = slice(d * width, (d + 1) * width)
                acc_ref[row, :, cols] += (
                    shifted(total[0:chan, cols], -1)
                    + total[chan : 2 * chan, cols]
                    + shifted(total[2 * chan :, cols], 1)
                )
    if split:
        kept = count // 2
        side = lax.axis_index("cout")
        mine_ref[...] = acc_ref[pl.ds(1 + side * kept, kept)].reshape(kept * chan, cells)
        sent = acc_ref[pl.ds(1 + (1 - side) * kept, kept)].reshape(kept * chan, cells)
        sent_ref[kept * chan : kept * chan + 8] = jnp.zeros((8, cells), F32)
        coded(sent_ref, 0, kept * chan + 8, sent)


def power(k):
    whole = k.astype(jnp.int32)
    size = jnp.abs(whole)
    out = jnp.ones(k.shape, F32)
    for i in range(7):
        step = jnp.where(whole > 0, 2.0 ** (2**i), 2.0 ** -(2**i))
        out = out * jnp.where((size >> i) & 1 == 1, step, 1.0)
    return out


def packed(out_ref, at, spot, x):
    rows, cols = x.shape
    most = jnp.max(jnp.max(jnp.abs(x), axis=0, keepdims=True), axis=1, keepdims=True)
    most = jnp.broadcast_to(jnp.maximum(most, 2.0**-100), (8, cols))
    k = 13.0 - jnp.floor(jnp.log2(most))
    out_ref[at : at + rows] = x * power(k)[0:1]
    out_ref[spot : spot + 8] = k


def unpacked(ref, at, rows, spot):
    return ref[at : at + rows] * power(-ref[spot : spot + 8])[0:1]


EDGE = 2.0**-3.5


def coded(out_ref, at, spot, x):
    rows, cols = x.shape
    size = jnp.abs(x)
    most = jnp.max(jnp.max(size, axis=0, keepdims=True), axis=1, keepdims=True)
    most = jnp.broadcast_to(jnp.maximum(most, 2.0**-100), (8, cols))
    k = 2.0 - jnp.floor(jnp.log2(most))
    root = size * (power(k)[0:1] * 1.96) + EDGE
    square = root * root
    square = square * square
    out_ref[at : at + rows] = jnp.where(x < 0.0, -square, square)
    out_ref[spot : spot + 8] = k


def decoded(ref, at, rows, spot):
    value = ref[at : at + rows]
    size = jnp.abs(value)
    root = size * lax.rsqrt(size)
    root = root * lax.rsqrt(root) - EDGE
    root = root * (power(-ref[spot : spot + 8])[0:1] * (1.0 / 1.96))
    return jnp.where(value < 0.0, -root, root)


def relay_kernel(plan, part_ref, *refs):
    back, rows_in, sums_in, rows_out = (plan[n] for n in ("back", "rows_in", "sums_in", "rows_out"))
    ins, outs = list(refs[: plan["ins"]]), list(refs[plan["ins"] + plan["skip"] :])
    full = part_ref.shape[0]
    mid = full // 2
    came = total = None
    if plan["raw"]:
        came = ins.pop(0)[...]
    if plan["unpack"]:
        ref = ins.pop(0)
        spot = ref.shape[0] - 16
        held = 0 if plan["raw"] else rows_in
        if held:
            came = unpacked(ref, 0, held, spot).astype(BF16)
        total = decoded(ref, held, sums_in, spot + 8)
    elif sums_in:
        total = ins.pop(0)[...]
    if sums_in == 0:
        total = part_ref[mid:] if back else part_ref[0:mid]
    elif sums_in == mid:
        pair = [total, jnp.zeros_like(total)]
        total = part_ref[...] + jnp.concatenate(pair[::-1] if back else pair, axis=0)
    else:
        total = part_ref[...] + total
    if rows_out:
        passed = came[rows_in - rows_out :] if back else came[0:rows_out]
        if plan["apart"]:
            outs.pop(0)[...] = passed
            rows_out = 0
    if plan["packs"]:
        out_ref = outs.pop(0)
        spot = out_ref.shape[0] - 16
        if rows_out and not plan["raw"]:
            start = rows_in - rows_out if back else 0
            out_ref[0:rows_out] = ref[start : start + rows_out]
            out_ref[spot : spot + 8] = ref[ref.shape[0] - 16 : ref.shape[0] - 8]
        elif rows_out:
            packed(out_ref, 0, spot, passed.astype(F32))
        else:
            out_ref[spot : spot + 8] = jnp.zeros((8, out_ref.shape[1]), F32)
        coded(out_ref, rows_out, spot + 8, total)
    else:
        outs.pop(0)[...] = total
    if outs:
        outs.pop(0)[...] = came


def mark_kernel(after_ref, token_ref, second_token_ref):
    token_ref[...] = jnp.zeros(token_ref.shape, F32)
    second_token_ref[...] = jnp.zeros(second_token_ref.shape, F32)


def stack_kernel(count, *refs):
    out_ref = refs[-1]
    for i in range(count):
        out_ref[i] = refs[i][...]


def join_kernel(first_ref, second_ref, out_ref):
    mid = first_ref.shape[0]
    out_ref[0:mid] = first_ref[...]
    out_ref[mid:] = second_ref[...]


def add_kernel(first_ref, *refs, skip=0):
    out_ref = refs[-1]
    total = first_ref[...]
    for ref in refs[: len(refs) - 1 - skip]:
        total = total + decoded(ref, 0, total.shape[0], total.shape[0] + 8)
    out_ref[...] = total.astype(BF16)


def call(kernel, out_shape, args, scratch=(), alias=None, flops=0):
    whole = pl.BlockSpec(memory_space=pltpu.VMEM)
    outs = jax.tree.map(lambda _: whole, out_shape)
    return pl.pallas_call(
        kernel,
        out_shape=jax.tree.map(lambda x: pltpu.VMEM(x.shape, x.dtype), out_shape),
        in_specs=[whole] * len(args),
        out_specs=outs,
        scratch_shapes=list(scratch),
        input_output_aliases=alias or {},
        compiler_params=pltpu.CompilerParams(vmem_limit_bytes=VMEM_LIMIT),
        cost_estimate=pl.CostEstimate(flops=flops, bytes_accessed=0, transcendentals=0),
    )(*args)


def per_device(features, kernel, grad_out):
    count, chan, slab, width = features.shape
    outs = kernel.shape[1]
    ring_size = lax.axis_size("cin")
    assert count == ring_size and slab == 2 and grad_out.shape[0] == 1 and lax.axis_size("depth") == 2
    cells = slab * width
    half = ring_size // 2
    mid = outs // 2
    ring = ring_of(ring_size)
    fwd = [(ring[i], ring[(i + 1) % ring_size]) for i in range(ring_size)]
    bwd = [(j, i) for i, j in fwd]
    swap = [(0, 1), (1, 0)]
    token = jax.ShapeDtypeStruct((8, cells), F32)

    def send(pair):
        return lax.ppermute(pair[0], "cin", fwd), lax.ppermute(pair[1], "cin", bwd)

    grads = [None] * ring_size
    own = lax.optimization_barrier(grad_out.reshape(outs, cells))
    grads[0] = own
    going = send((own, own))

    feat = features.transpose(0, 2, 1, 3)
    layer = [jax.ShapeDtypeStruct((n, chan, width), BF16) for n in (count // 2, count // 2, count)]
    got = [lax.ppermute(x, "depth", swap) for x in call(split_kernel, layer, (feat,))]
    taps = kernel.transpose(0, 2, 1).reshape(3, 9 * chan, outs)
    ext_shape = jax.ShapeDtypeStruct((count + 2, 3 * chan, cells + 2 * width), BF16)
    ext = call(functools.partial(extend_kernel, True), ext_shape, (feat, *got[:2]))
    w_out = call(turn_kernel, jax.ShapeDtypeStruct((3, outs, 9 * chan), BF16), (taps, ext))
    ext_other = call(functools.partial(extend_kernel, False), ext_shape, (feat, *got))

    def forward(offsets, after=()):
        return call(
            functools.partial(forward_kernel, offsets, len(after), width),
            [jax.ShapeDtypeStruct((outs, cells), F32)] * len(offsets),
            (ext, w_out, *after),
        )

    def weight_part(group, mine, theirs, acc, after):
        *acc, token_f, token_b = call(
            functools.partial(weight_kernel, group, width, 1.0, not acc, False, range(3)),
            [jax.ShapeDtypeStruct((9 * chan, outs), F32)] * 3 + [token, token],
            (ext, ext_other, mine, theirs, *acc, after),
        )
        return acc, (token_f, token_b)

    def weight_last(group, mine, theirs, acc, after, depths, made):
        shape = (3, 9 * chan, outs)
        scale = 1.0 / math.sqrt(count * cells * lax.axis_size("depth"))
        whole = pl.BlockSpec(memory_space=pltpu.VMEM)
        anywhere = pl.BlockSpec(memory_space=pl.ANY)
        args = (ext, ext_other, mine, theirs, *acc, after, *made)
        size = len(depths)
        return pl.pallas_call(
            functools.partial(weight_kernel, group, width, scale, False, True, depths),
            out_shape=jax.ShapeDtypeStruct(shape, F32),
            in_specs=[whole] * (len(args) - len(made)) + [anywhere] * len(made),
            out_specs=anywhere,
            scratch_shapes=[pltpu.VMEM((size, *shape[1:]), F32), pltpu.SemaphoreType.DMA((size,))],
            input_output_aliases={len(args) - 1: 0} if made else {},
            compiler_params=pltpu.CompilerParams(vmem_limit_bytes=VMEM_LIMIT),
            cost_estimate=pl.CostEstimate(flops=0, bytes_accessed=0, transcendentals=0),
        )(*args)

    parts = lax.axis_size("cout")

    def input_part(group, theirs, back, split):
        held = [grads[k] for k in group]
        first = back is None
        size = len(group)
        args = (taps, theirs, *held)
        whole = jax.ShapeDtypeStruct((count + 2, chan, cells), F32)
        kept = jax.ShapeDtypeStruct((count // 2 * chan, cells), F32)
        sent = jax.ShapeDtypeStruct((count // 2 * chan + 16, cells), F32)
        pad = pltpu.VMEM((size, outs, cells + 2 * width), BF16)
        return call(
            functools.partial(input_kernel, group, first, count, split),
            [kept, sent] if split else [whole, token],
            args if first else (*args, back),
            scratch=[pltpu.VMEM(whole.shape, F32), pad] if split else [pad],
        )

    part = [None] * ring_size
    (part[half],) = forward([half])
    others = [k for k in range(ring_size) if k != half]
    near = [0, ring_size - 1, 1, ring_size - 2, 2]
    far = [k for k in range(ring_size) if k not in near]

    row = jax.ShapeDtypeStruct((outs, cells), BF16)
    back = None
    acc = []
    tokens = []
    going = [[x] for x in going]
    sums = [[], []]
    for r in range(1, half + 1):
        rows_in = mid if r == half else outs
        rows_out = 0 if r == half else mid if r + 1 == half else outs
        sums_in = 0 if r == 1 else mid if r == 2 else outs
        sums_out = mid if r == 1 else outs
        unpack = r > 1
        packs = True
        raw = r <= 2 or not unpack
        apart = rows_out if r == 1 or not packs else 0
        group = near if r == 2 else far if r == half else []
        if r == 2:
            for k, p in zip(others, forward(others, [x for pair in sent_on for x in pair])):
                part[k] = p
        left = half + 1 - r
        kept, sent_on = [], []
        for i, perm in ((0, fwd), (1, bwd)):
            ins = going[i] if raw else []
            if unpack:
                late = tokens[i][0:1] if tokens else 0.0
                ins = ins + [sums[i][0].astype(F32) + late]
            else:
                ins = ins + sums[i]
            shapes = [jax.ShapeDtypeStruct((apart, cells), BF16)] if apart else []
            if packs:
                packed_rows = rows_out - apart + sums_out + 16
                shapes = shapes + [jax.ShapeDtypeStruct((packed_rows, cells), F32)]
            else:
                shapes = shapes + [jax.ShapeDtypeStruct((sums_out, cells), F32)]
            sent = len(shapes)
            if rows_in and not raw:
                shapes = shapes + [jax.ShapeDtypeStruct((rows_in, cells), BF16)]
            plan = dict(
                back=bool(i),
                raw=raw,
                rows_in=rows_in,
                sums_in=sums_in,
                rows_out=rows_out,
                apart=apart,
                packs=packs,
                unpack=unpack,
                ins=len(ins),
                skip=0,
            )
            term = part[ring_size - left if i else left]
            relay = functools.partial(relay_kernel, plan)
            made = call(relay, shapes, (term, *ins))
            kept.append(going[i][0] if raw else made[-1])
            total = made[sent - 1]
            sent_on.append([total])
            if packs:
                total = total.astype(jnp.float16)
            going[i] = [lax.ppermute(x, "cin", perm) for x in made[: sent - 1]]
            sums[i] = [lax.ppermute(total, "cin", perm)]
        if r == half:
            grads[half] = call(join_kernel, row, kept)
        else:
            grads[ring_size - r], grads[r] = kept
        tokens = []
        if group:
            size = len(group)
            stack = jax.ShapeDtypeStruct((size, outs, cells), BF16)
            mine = [grads[k] for k in group]
            mine = call(functools.partial(stack_kernel, size), stack, (*mine, *[x for pair in sent_on for x in pair]))
            theirs = lax.ppermute(mine, "depth", swap)
            back, token_i = input_part(group, theirs, back, r == half and parts == 2)
            if r == half:
                tokens = call(mark_kernel, [token, token], (back,))
                kernel_grad = weight_last(group, mine, theirs, acc, tokens[0], range(3), ())
            else:
                acc, tokens = weight_part(group, mine, theirs, acc, token_i)
    (f,), (b,) = sums

    kernel_grad = kernel_grad.reshape(27, chan, outs).transpose(0, 2, 1)
    if parts == 2:
        other = lax.ppermute(token_i.astype(jnp.float16), "cout", swap).astype(F32)
        terms = [back, other]
    else:
        back = back[1 : count + 1]
        terms = [lax.psum_scatter(back, "cout", scatter_dimension=0, tiled=True)]
        terms = [terms[0].reshape(count // parts * chan, cells)]
    input_grad = call(
        add_kernel,
        jax.ShapeDtypeStruct((count // parts * chan, cells), BF16),
        tuple(terms),
    )
    input_grad = input_grad.reshape(count // parts, chan, slab, width)
    output = call(
        functools.partial(add_kernel, skip=1),
        jax.ShapeDtypeStruct((outs, cells), BF16),
        (part[0], f.astype(F32) + tokens[0][0:1], b.astype(F32) + tokens[1][0:1], input_grad),
    )
    output = output.reshape(1, outs, slab, width)
    return (output, input_grad, kernel_grad)


def solution(mesh):
    return jax.shard_map(
        per_device,
        mesh=mesh,
        in_specs=(
            P(None, "cin", "depth", None),
            P(None, "cout", "cin"),
            P("cin", "cout", "depth", None),
        ),
        out_specs=(
            P("cin", "cout", "depth", None),
            P("cout", "cin", "depth", None),
            P(None, "cout", "cin"),
        ),
        check_vma=False,
    )
```
